128 devices in a mesh: section: 4 (over z_lo, core), dp: 32 (over x, z_hi, y).
Axes of the slice: x: 4, y: 4, z: 4 (z_hi: 2, z_lo: 2; z = z_hi * 2 + z_lo), core: 2. Of those that a mesh axis runs over, the one named last changes fastest.
Arguments:
- inputs: bfloat16 [2, 64, 64, 6656], P(None, 'dp'), may hold values from -6 to 6
- cotangent: bfloat16 [2, 64, 64, 6656], P(None, 'dp'), may hold values from -6 to 6
- stored: bfloat16 [3, 128, 64, 6656], P(None, 'dp'), may hold values from -6 to 6
- sample_ids: int32 [2, 64], P(None, 'dp'), may hold values from 0 to 127, as said below
- act_exp: int32 [3, 2, 64, 64, 52], P(None, None, 'dp'), may hold values from -4 to 0
- grad_exp: int32 [3, 2, 64, 64, 52], P(None, None, 'dp'), may hold values from -7 to -3
- gain: float32 [4, 6656], P('section'), may hold values from 0.1 to 1.9
- down_weight: bfloat16 [4, 6656, 256], P('section'), may hold values from -0.078125 to 0.078125
- up_weight: bfloat16 [4, 6656, 256], P('section'), may hold values from -0.375 to 0.375
Outputs:
- grad_gain: float32 [4, 6656], P('section')
- grad_down: float32 [4, 6656, 256], P('section', 'dp')
- grad_up: float32 [4, 6656, 256], P('section', 'dp')
The draws below stay inside these ranges and needn't reach their ends.
Inputs may be any that keep to these rules, and one draw needn't show every extreme that they name: `sample_ids`: for each j, the ids in columns j * 2 to (j + 1) * 2 - 1 of all micro-batches together are the numbers j * 4 to (j + 1) * 4 - 1, each once.
All inputs are finite; a program needn't handle non-finite values.
Results may differ from the reference program's by a relative error of at most 0.015.
Values may be sent and summed in bfloat16 or wider, within the bound.
A program may use at most 320 MiB of HBM per device.

```python
import jax
import jax.numpy as jnp
from jax import lax

D = 6656
R = 256
SEQ = 64
SPM = 2
MICRO = 2
SAMPLES = 64
POOL = 128
BOUNDS = 3
NBLK = 52
N_SECTION = 4


def draw_sample_ids(key, part):
    key = jax.random.fold_in(key, 5)
    groups = SAMPLES // SPM
    keys = jax.random.split(key, groups)
    perms = jax.vmap(lambda single: jax.random.permutation(single, MICRO * SPM))(keys)
    offsets = (jnp.arange(groups, dtype=jnp.int32) * (MICRO * SPM))[:, None]
    ids = perms.astype(jnp.int32) + offsets
    ids = ids.reshape(groups, MICRO, SPM).transpose(1, 0, 2).reshape(MICRO, SAMPLES)
    return ids.astype(jnp.int32)


def touch_ends(result, stream_key, least, high):
    place = [jax.random.randint(jax.random.fold_in(stream_key, axis), (), 0, length) for axis, length in enumerate(result.shape)]
    longest = result.shape.index(max(result.shape))
    beside = place[:longest] + [(place[longest] + 1) % result.shape[longest]] + place[longest + 1:]
    return result.at[tuple(place)].set(least).at[tuple(beside)].set(high)


def levels(rng, extent, shards, smallest, high):
    loudness, own = 1.0, jax.random.fold_in(rng, 6)
    for position, shards_of in shards:
        steps = jnp.exp(jax.random.uniform(jax.random.fold_in(own, position), (shards_of,), jnp.float32, smallest / len(shards), high / len(shards)))
        loudness = loudness * jnp.repeat(steps, extent[position] // shards_of).reshape([-1 if axis == position else 1 for axis in range(len(extent))])
    return loudness


def centred(key, extent, width, reach, shards=(), kind=jnp.bfloat16):
    result = width * jax.random.normal(key, extent, jnp.float32)
    if shards:
        result = result * levels(key, extent, shards, -0.22, 0.18)
    return jnp.clip(result, -reach, reach).astype(kind)


def setup_inputs(seed: int = 0) -> dict:
    key_of = jax.random.split(jax.random.key(seed), 10)
    return {
        "inputs": centred(key_of[0], (MICRO, SAMPLES, SEQ, D), 1.0, 6.0, ((1, 32),)),
        "cotangent": centred(key_of[1], (MICRO, SAMPLES, SEQ, D), 1.0, 6.0, ((1, 32),)),
        "stored": centred(key_of[2], (BOUNDS, POOL, SEQ, D), 1.0, 6.0, ((1, 32),)),
        "sample_ids": draw_sample_ids(jax.random.fold_in(key_of[9], 71), 0),
        "act_exp": touch_ends(jax.random.randint(key_of[4], (BOUNDS, MICRO, SAMPLES, SEQ, NBLK), -4, 1), jax.random.fold_in(key_of[4], 1), -4, 0).astype(jnp.int32),
        "grad_exp": touch_ends(jax.random.randint(key_of[5], (BOUNDS, MICRO, SAMPLES, SEQ, NBLK), -7, -2), jax.random.fold_in(key_of[5], 1), -7, (-2) - 1).astype(jnp.int32),
        "gain": jnp.clip(1.0 + 0.18 * jax.random.normal(key_of[6], (N_SECTION, D), jnp.float32), 0.1, 1.9),
        "down_weight": centred(key_of[7], (N_SECTION, D, R), D ** -0.5, 0.078125, ((0, 4),)),
        "up_weight": centred(key_of[8], (N_SECTION, D, R), R ** -0.5, 0.375, ((0, 4),)),
    }


EPS = 1e-05

def power_two(exps):
    return jnp.left_shift(jnp.ones_like(exps), exps + 8).astype(jnp.float32) / 256.0

def blockwise(values, factor):
    count = values.shape[0]
    return (values.reshape(count, factor.shape[1], -1) * factor[:, :, None]).reshape(count, -1)

def norm_parts(x_in, gain_row):
    recip = lax.rsqrt(lax.optimization_barrier(jnp.mean(x_in * x_in, axis=-1, keepdims=True)) + EPS)
    normed = x_in * recip
    return (recip, normed, (normed * gain_row).astype(jnp.bfloat16))

def reference(inputs, cotangent, stored, sample_ids, act_exp, grad_exp, gain, down_weight, up_weight):
    stations = gain.shape[0]
    rows = SAMPLES * SEQ
    saved = []
    for micro in range(MICRO):
        x_in = inputs[micro].reshape(rows, D).astype(jnp.float32)
        keep = []
        for station in range(stations):
            keep.append(x_in)
            if station + 1 < stations:
                recip, normed, xn = norm_parts(x_in, gain[station])
                pre = jnp.dot(xn, down_weight[station], preferred_element_type=jnp.float32)
                hidden = jax.nn.silu(pre).astype(jnp.bfloat16)
                y_out = x_in + jnp.dot(hidden, up_weight[station].T, preferred_element_type=jnp.float32)
                base = stored[station][sample_ids[micro]].reshape(rows, D).astype(jnp.float32)
                expo = act_exp[station, micro].reshape(rows, NBLK)
                scale = power_two(expo)
                code = jnp.clip(blockwise(y_out - base, 1.0 / scale), -8.0, 7.0).astype(jnp.bfloat16)
                x_in = base + blockwise(code.astype(jnp.float32), scale)
        saved.append(keep)
    g_gain = [jnp.zeros((D,), jnp.float32) for s in range(stations)]
    g_down = [jnp.zeros((D, R), jnp.float32) for s in range(stations)]
    g_up = [jnp.zeros((D, R), jnp.float32) for s in range(stations)]
    for micro in range(MICRO):
        grad_y = cotangent[micro].reshape(rows, D).astype(jnp.float32)
        for station in reversed(range(stations)):
            x_in = saved[micro][station]
            recip, normed, xn = norm_parts(x_in, gain[station])
            pre = jnp.dot(xn, down_weight[station], preferred_element_type=jnp.float32)
            hidden = jax.nn.silu(pre).astype(jnp.bfloat16)
            dyb = grad_y.astype(jnp.bfloat16)
            dh = jnp.dot(dyb, up_weight[station], preferred_element_type=jnp.float32)
            sig = jax.nn.sigmoid(pre)
            dpre = (dh * sig * (1.0 + pre * (1.0 - sig))).astype(jnp.bfloat16)
            g_up[station] = g_up[station] + jnp.dot(dyb.T, hidden, preferred_element_type=jnp.float32)
            g_down[station] = g_down[station] + jnp.dot(xn.T, dpre, preferred_element_type=jnp.float32)
            dxn = jnp.dot(dpre, down_weight[station].T, preferred_element_type=jnp.float32)
            g_gain[station] = g_gain[station] + lax.optimization_barrier(jnp.sum(dxn * normed, axis=0))
            dz = dxn * gain[station]
            grad_x = recip * (dz - normed * lax.optimization_barrier(jnp.mean(dz * normed, axis=-1, keepdims=True))) + grad_y
            if station > 0:
                scale = power_two(grad_exp[station - 1, micro].reshape(rows, NBLK))
                code = jnp.clip(blockwise(grad_x, 1.0 / scale), -128.0, 127.0).astype(jnp.bfloat16)
                grad_y = blockwise(code.astype(jnp.float32), scale)
    factor = 1.0 / jnp.sqrt(jnp.float32(MICRO * SAMPLES * SEQ))
    return (jnp.stack(g_gain) * factor, jnp.stack(g_down) * factor, jnp.stack(g_up) * factor)
```

```python
import functools
import math

import jax
import jax.numpy as jnp
from jax import lax
from jax.experimental import pallas as pl
from jax.experimental.pallas import tpu as pltpu
from jax.sharding import PartitionSpec as P

EPS = 1e-05
MESH = pl.DeviceIdType.MESH
F32 = jnp.float32
BF16 = jnp.bfloat16
C = 32
TW = 512
NX, NZ, NY = 4, 2, 4
BR = 208


def dot_nn(a, b):
    return jnp.dot(a, b, preferred_element_type=F32)


def dot_nt(a, b):
    return lax.dot_general(a, b, (((1,), (1,)), ((), ())), preferred_element_type=F32)


def dot_tn(a, b):
    return lax.dot_general(a, b, (((0,), (0,)), ((), ())), preferred_element_type=F32)


def kernel(
    factor,
    ids_ref, inputs, cotangent, stored, act_exp, grad_exp, gain, down, up,
    out_gain, out_down, out_up,
    x_st, dyb_st, xn_st, xout, dyout, down_v, up_v, stored_v, ascale, gscale,
    act_v, grad_v, gain_v, pad_v, r_st, p_st, h_st, dp_st, ybuf, gg,
    g0, g1, rel0, rel1, frl0, frl1, p1_0, p1_1, rel2, frl2, p2, zrecv, gx,
    load_sem, xin_sem, xs_sem, dy_sem, ds_sem, rs_send, rs_recv, gs_send, gs_recv, z_send, z_recv,
):
    tokens, width = x_st.shape
    nchunk = tokens // C
    seq = inputs.shape[2]
    per = seq // C
    ntile = width // TW
    s = lax.axis_index("section")
    dp = lax.axis_index("dp")
    xc = lax.div(dp, NZ * NY)
    zc = lax.rem(lax.div(dp, NY), NZ)
    yc = lax.rem(dp, NY)
    last = lax.axis_size("section") - 1

    def at_x(t):
        return t * (NZ * NY) + zc * NY + yc

    def at_y(t):
        return xc * (NZ * NY) + zc * NY + t

    zmate = xc * (NZ * NY) + (1 - zc) * NY + yc

    loads = [
        pltpu.make_async_copy(act_exp.at[jnp.minimum(s, last - 1)], act_v, load_sem.at[0]),
        pltpu.make_async_copy(gain, gain_v, load_sem.at[1]),
        pltpu.make_async_copy(down.at[0], down_v, load_sem.at[2]),
        pltpu.make_async_copy(up.at[0], up_v, load_sem.at[3]),
        pltpu.make_async_copy(stored.at[jnp.minimum(s, last - 1)], stored_v, load_sem.at[4]),
        pltpu.make_async_copy(grad_exp.at[jnp.maximum(s - 1, 0)], grad_v, load_sem.at[5]),
    ]
    loads[0].start()
    loads[1].start()

    def rows_of(c):
        return pl.ds(pl.multiple_of(c * C, C), C)

    def own_rows(source, stash, sem):
        for c in range(nchunk):
            slot = c // per
            pltpu.make_async_copy(
                source.at[slot // 2, slot % 2, pl.ds((c % per) * C, C)],
                stash.at[pl.ds(c * C, C)],
                sem.at[c],
            ).start()

    @pl.when(s == 0)
    def _():
        own_rows(inputs, x_st, xin_sem)

    for load in loads[2:]:
        load.start()

    @pl.when(s == last)
    def _():
        own_rows(cotangent, dyb_st, dy_sem)

    barrier = pltpu.get_barrier_semaphore()
    for t in range(1, NX):
        pl.semaphore_signal(
            barrier, inc=1, device_id={"dp": at_x(lax.rem(xc + t, NX))}, device_id_type=MESH
        )
        pl.semaphore_signal(
            barrier, inc=1, device_id={"dp": at_y(lax.rem(yc + t, NY))}, device_id_type=MESH
        )
    pl.semaphore_signal(barrier, inc=1, device_id={"dp": zmate}, device_id_type=MESH)

    @pl.when(s > 0)
    def _():
        pl.semaphore_signal(barrier, inc=1, device_id={"section": s - 1}, device_id_type=MESH)

    @pl.when(s < last)
    def _():
        pl.semaphore_signal(barrier, inc=1, device_id={"section": s + 1}, device_id_type=MESH)

    def expand(exps, out):
        scale = jnp.left_shift(jnp.ones(exps.shape, jnp.int32), exps[...] + 8).astype(F32) / 256.0
        pad_v[...] = jnp.zeros_like(pad_v)
        pad_v[:, : exps.shape[-1]] = scale.reshape(tokens, exps.shape[-1]).astype(BF16)

        def tile(k, carry):
            cols = pl.ds(pl.multiple_of(k * TW, TW), TW)
            block = lax.broadcasted_iota(jnp.int32, (pad_v.shape[1], TW), 0)
            lane = lax.broadcasted_iota(jnp.int32, (pad_v.shape[1], TW), 1)
            pick = (block == k * (TW // 128) + jnp.right_shift(lane, 7)).astype(F32).astype(BF16)
            out[:, cols] = dot_nn(pad_v[...], pick).astype(BF16)
            return carry

        lax.fori_loop(0, ntile, tile, 0)

    loads[0].wait()
    expand(act_v, ascale)
    gg[...] = jnp.zeros_like(gg)
    loads[5].wait()
    expand(grad_v, gscale)
    for load in loads[1:5]:
        load.wait()

    npeer = NX - 1 + NY - 1 + 1
    pl.semaphore_wait(barrier, npeer + jnp.where(s > 0, 1, 0) + jnp.where(s < last, 1, 0))

    def send_x(c):
        return pltpu.make_async_remote_copy(
            src_ref=xout.at[rows_of(c)], dst_ref=x_st.at[rows_of(c)],
            send_sem=xs_sem.at[c], recv_sem=xin_sem.at[c],
            device_id={"section": s + 1}, device_id_type=MESH,
        )

    def send_dy(c):
        return pltpu.make_async_remote_copy(
            src_ref=dyout.at[rows_of(c)], dst_ref=dyb_st.at[rows_of(c)],
            send_sem=ds_sem.at[c], recv_sem=dy_sem.at[c],
            device_id={"section": s - 1}, device_id_type=MESH,
        )

    def cols_of(k):
        return pl.ds(pl.multiple_of(k * TW, TW), TW)

    def forward(c):
        rows = rows_of(c)
        pltpu.make_async_copy(x_st.at[rows], x_st.at[rows], xin_sem.at[c]).wait()

        def square(k, acc):
            x = x_st[rows, cols_of(k)].astype(F32)
            return acc + x * x

        acc = lax.fori_loop(0, ntile, square, jnp.zeros((C, TW), F32), unroll=True)
        recip = lax.rsqrt(jnp.sum(acc, axis=1, keepdims=True) / width + EPS)
        r_st[rows, :] = jnp.broadcast_to(recip, (C, 128))
        wide = jnp.broadcast_to(recip, (C, TW))

        def norm(k, carry):
            x = x_st[rows, cols_of(k)].astype(F32)
            xn_st[rows, cols_of(k)] = (x * wide * gain_v[:, cols_of(k)]).astype(BF16)
            return carry

        lax.fori_loop(0, ntile, norm, 0, unroll=True)
        pre = dot_nn(xn_st[rows, :], down_v[...])
        hidden = (pre * jax.nn.sigmoid(pre)).astype(BF16)
        p_st[rows, :] = pre
        h_st[rows, :] = hidden

        @pl.when(s < last)
        def _():
            ybuf[...] = dot_nt(hidden, up_v[...])
            slot = lax.div(c, per)
            pos = pl.ds(pl.multiple_of(lax.rem(c, per) * C, C), C)
            own = ids_ref[lax.div(slot, 2), lax.rem(slot, 2)] - dp * stored_v.shape[0]
            own = jnp.clip(own, 0, stored_v.shape[0] - 1)

            def code(k, carry):
                cols = cols_of(k)
                y = x_st[rows, cols].astype(F32) + ybuf[:, cols]
                base = stored_v[own, pos, cols].astype(F32)
                scale = ascale[rows, cols].astype(F32)
                step = jnp.clip(y - base, -8.0 * scale, 7.0 * scale)
                xout[rows, cols] = (base + step).astype(BF16)
                return carry

            lax.fori_loop(0, ntile, code, 0, unroll=True)
            send_x(c).start()

    def backward(c):
        rows = rows_of(c)
        pltpu.make_async_copy(dyb_st.at[rows], dyb_st.at[rows], dy_sem.at[c]).wait()
        dh = dot_nn(dyb_st[rows, :], up_v[...])
        pre = p_st[rows, :]
        sig = jax.nn.sigmoid(pre)
        dpre = (dh * sig * (1.0 + pre * (1.0 - sig))).astype(BF16)
        dp_st[rows, :] = dpre
        ybuf[...] = dot_nt(dpre, down_v[...])
        wide = jnp.concatenate([r_st[rows, :]] * (TW // 128), axis=1)

        def first(k, acc):
            cols = cols_of(k)
            prod = ybuf[:, cols] * (x_st[rows, cols].astype(F32) * wide)
            gg[:, cols] += jnp.sum(prod.reshape(C // 8, 8, TW), axis=0)
            return acc + prod * gain_v[:, cols]

        acc = lax.fori_loop(0, ntile, first, jnp.zeros((C, TW), F32), unroll=True)

        @pl.when(s > 0)
        def _():
            mean = jnp.broadcast_to(jnp.sum(acc, axis=1, keepdims=True) / width, (C, TW))

            def second(k, carry):
                cols = cols_of(k)
                z = x_st[rows, cols].astype(F32) * wide
                dz = ybuf[:, cols] * gain_v[:, cols]
                grad = wide * (dz - z * mean) + dyb_st[rows, cols].astype(F32)
                scale = gscale[rows, cols].astype(F32)
                dyout[rows, cols] = jnp.clip(grad, -128.0 * scale, 127.0 * scale).astype(BF16)
                return carry

            lax.fori_loop(0, ntile, second, 0, unroll=True)
            send_dy(c).start()

    lag = jnp.where(s == last, 0, jnp.where(s == last - 1, 2, nchunk))

    def step(t, carry):
        @pl.when(t < nchunk)
        def _():
            forward(t)

        @pl.when((t >= lag) & (t < lag + nchunk))
        def _():
            backward(t - lag)

        return carry

    lax.fori_loop(0, 2 * nchunk, step, 0)

    nrow = width // 128
    for b in range(nrow):
        gx[0, xc, b : b + 1, :] = jnp.sum(gg[:, b * 128 : (b + 1) * 128], axis=0, keepdims=True)

    def gain_send(phase, t):
        coord, at = ((xc, at_x), (yc, at_y))[phase]
        return pltpu.make_async_remote_copy(
            src_ref=gx.at[phase, coord], dst_ref=gx.at[phase, coord],
            send_sem=gs_send.at[phase, t], recv_sem=gs_recv.at[phase, coord],
            device_id={"dp": at(lax.rem(coord + t, 4))}, device_id_type=MESH,
        )

    def gain_wait(phase):
        coord = (xc, yc)[phase]
        for t in range(1, 4):
            other = lax.rem(coord + t, 4)
            pltpu.make_async_copy(
                gx.at[phase, other], gx.at[phase, other], gs_recv.at[phase, other]
            ).wait()

    def gain_sum(phase):
        return (gx[phase, 0] + gx[phase, 1]) + (gx[phase, 2] + gx[phase, 3])

    for t in range(1, 4):
        gain_send(0, t).start()

    part = NZ * NY * BR

    def grads(stash, units, out):
        def tile(k, carry):
            cols = pl.ds(pl.multiple_of(k * part, 128), part)
            value = dot_tn(stash[:, cols], units[...]).astype(BF16)
            out[0, k] = value[:, :128].reshape(NZ, NY, BR, 128)
            out[1, k] = value[:, 128:].reshape(NZ, NY, BR, 128)
            return carry

        lax.fori_loop(0, NX, tile, 0)

    def ring_sends(kind, phase, chunk, rel, frl, coord, at):
        right, left, opp = lax.rem(coord + 1, 4), lax.rem(coord + 3, 4), lax.rem(coord + 2, 4)

        def copy(i, src, dst, to):
            return pltpu.make_async_remote_copy(
                src_ref=src, dst_ref=dst,
                send_sem=rs_send.at[kind, phase, i], recv_sem=rs_recv.at[kind, phase, i],
                device_id={"dp": at(to)}, device_id_type=MESH,
            )

        return [
            copy(0, chunk(0, opp), rel.at[0], right),
            copy(1, chunk(1, opp), rel.at[1], left),
            copy(2, chunk(1, right), frl.at[0, 1], right),
            copy(3, chunk(0, left), frl.at[1, 0], left),
            copy(4, chunk(0, right), frl.at[0, 0], right),
            copy(5, chunk(1, left), frl.at[1, 1], left),
        ]

    sends = {}
    sends[0, 0] = ring_sends(0, 0, lambda a, t: g0.at[a, t], rel0, frl0, xc, at_x)
    sends[1, 0] = ring_sends(1, 0, lambda a, t: g1.at[a, :, :, t], rel1, frl1, yc, at_y)
    sends[0, 1] = ring_sends(
        0, 1, lambda a, t: p1_0.at[a, :, t], rel2.at[0], frl2.at[0], yc, at_y
    )
    sends[1, 1] = ring_sends(
        1, 1, lambda a, t: p1_1.at[a, t], rel2.at[1], frl2.at[1], xc, at_x
    )

    def add(*refs):
        total = refs[0][...].astype(F32)
        for ref in refs[1:]:
            total = total + ref[...].astype(F32)
        return total

    right_x, left_x = lax.rem(xc + 1, 4), lax.rem(xc + 3, 4)
    right_y, left_y = lax.rem(yc + 1, 4), lax.rem(yc + 3, 4)

    def loop(n, body):
        def run(i, carry):
            body(i)
            return carry

        lax.fori_loop(0, n, run, 0)

    grads(dyb_st, h_st, g1)
    for i in range(4):
        sends[1, 0][i].start()
    grads(xn_st, dp_st, g0)
    for i in range(4):
        sends[0, 0][i].start()

    for a, to in ((0, right_y), (1, left_y)):
        sends[1, 0][a].wait_recv()

        def relay1(i, a=a, to=to):
            u, v = lax.div(i, NZ), lax.rem(i, NZ)
            g1[a, u, v, to] = add(g1.at[a, u, v, to], rel1.at[a, u, v]).astype(BF16)

        loop(NX * NZ, relay1)
        sends[1, 0][4 + a].start()
    for a, to in ((0, right_x), (1, left_x)):
        sends[0, 0][a].wait_recv()

        def relay0(i, a=a, to=to):
            u, v = lax.div(i, NY), lax.rem(i, NY)
            g0[a, to, u, v] = add(g0.at[a, to, u, v], rel0.at[a, u, v]).astype(BF16)

        loop(NZ * NY, relay0)
        sends[0, 0][4 + a].start()

    gain_wait(0)
    gx[1, yc] = gain_sum(0)
    for t in range(1, 4):
        gain_send(1, t).start()

    for i in range(2, 6):
        sends[1, 0][i].wait_recv()

    def own1(i):
        a, u, v = lax.div(i, NX * NZ), lax.rem(lax.div(i, NZ), NX), lax.rem(i, NZ)
        p1_1[a, u, v] = add(
            g1.at[a, u, v, yc], frl1.at[0, a, u, v], frl1.at[1, a, u, v]
        ).astype(BF16)

    loop(2 * NX * NZ, own1)
    for i in range(4):
        sends[1, 1][i].start()
    for i in range(2, 6):
        sends[0, 0][i].wait_recv()

    def own0(i):
        a, u, v = lax.div(i, NZ * NY), lax.rem(lax.div(i, NY), NZ), lax.rem(i, NY)
        p1_0[a, u, v] = add(
            g0.at[a, xc, u, v], frl0.at[0, a, u, v], frl0.at[1, a, u, v]
        ).astype(BF16)

    loop(2 * NZ * NY, own0)
    for i in range(4):
        sends[0, 1][i].start()

    for a, to in ((0, right_x), (1, left_x)):
        sends[1, 1][a].wait_recv()

        def relay3(v, a=a, to=to):
            p1_1[a, to, v] = add(p1_1.at[a, to, v], rel2.at[1, a, v]).astype(BF16)

        loop(NZ, relay3)
        sends[1, 1][4 + a].start()
    for a, to in ((0, right_y), (1, left_y)):
        sends[0, 1][a].wait_recv()

        def relay2(v, a=a, to=to):
            p1_0[a, v, to] = add(p1_0.at[a, v, to], rel2.at[0, a, v]).astype(BF16)

        loop(NZ, relay2)
        sends[0, 1][4 + a].start()

    gain_wait(1)
    gx[2, zc] = gain_sum(1)

    def mate(i, ref_src, ref_dst):
        return pltpu.make_async_remote_copy(
            src_ref=ref_src, dst_ref=ref_dst, send_sem=z_send.at[i], recv_sem=z_recv.at[i],
            device_id={"dp": zmate}, device_id_type=MESH,
        )

    zgain = mate(2, gx.at[2, zc], gx.at[2, zc])
    zgain.start()

    zsend = {}
    for kind in (1, 0):
        for i in range(2, 6):
            sends[kind, 1][i].wait_recv()
        for a in range(2):
            if kind == 0:
                mine = add(p1_0.at[a, 1 - zc, yc], frl2.at[0, 0, a, 1 - zc], frl2.at[0, 1, a, 1 - zc])
            else:
                mine = add(p1_1.at[a, xc, 1 - zc], frl2.at[1, 0, a, 1 - zc], frl2.at[1, 1, a, 1 - zc])
            p2[kind, a] = mine.astype(BF16)
        zsend[kind] = mate(kind, p2.at[kind], zrecv.at[kind])
        zsend[kind].start()

    for kind, out in ((1, out_up), (0, out_down)):
        zsend[kind].wait_recv()
        for a in range(2):
            if kind == 0:
                mine = add(
                    p1_0.at[a, zc, yc], frl2.at[0, 0, a, zc], frl2.at[0, 1, a, zc], zrecv.at[0, a]
                )
            else:
                mine = add(
                    p1_1.at[a, xc, zc], frl2.at[1, 0, a, zc], frl2.at[1, 1, a, zc], zrecv.at[1, a]
                )
            out[:, a * 128 : (a + 1) * 128] = mine * factor

    pltpu.make_async_copy(gx.at[2, 1 - zc], gx.at[2, 1 - zc], z_recv.at[2]).wait()
    out_gain[...] = (gx[2, 0] + gx[2, 1]) * factor

    zgain.wait_send()
    for kind in (0, 1):
        zsend[kind].wait_send()
        for phase in (0, 1):
            for i in range(6):
                sends[kind, phase][i].wait_send()
    for phase in (0, 1):
        for t in range(1, 4):
            gain_send(phase, t).wait_send()

    @pl.when(s < last)
    def _():
        loop(nchunk, lambda c: send_x(c).wait_send())

    @pl.when(s > 0)
    def _():
        loop(nchunk, lambda c: send_dy(c).wait_send())


def local(inputs, cotangent, stored, sample_ids, act_exp, grad_exp, gain, down_weight, up_weight):
    micro, spm, seq, width = inputs.shape
    tokens = micro * spm * seq
    units = down_weight.shape[2]
    nblk = act_exp.shape[4]
    nchunk = tokens // C
    ndp = lax.axis_size("dp")
    factor = 1.0 / math.sqrt(tokens * ndp)
    hbm = pl.BlockSpec(memory_space=pl.ANY)
    vmem = pl.BlockSpec(memory_space=pltpu.VMEM)
    big = pltpu.VMEM((tokens, width), BF16)
    dma = pltpu.SemaphoreType.DMA
    scratch = [
        big, big, big, big, big,
        pltpu.VMEM((width, units), BF16), pltpu.VMEM((width, units), BF16),
        pltpu.VMEM(stored.shape[1:], BF16),
        big, big,
        pltpu.VMEM(act_exp.shape[1:], jnp.int32), pltpu.VMEM(grad_exp.shape[1:], jnp.int32),
        pltpu.VMEM((1, width), F32),
        pltpu.VMEM((tokens, 128), BF16),
        pltpu.VMEM((tokens, 128), F32),
        pltpu.VMEM((tokens, units), F32),
        pltpu.VMEM((tokens, units), BF16),
        pltpu.VMEM((tokens, units), BF16),
        pltpu.VMEM((C, width), F32),
        pltpu.VMEM((8, width), F32),
        pltpu.VMEM((2, NX, NZ, NY, BR, 128), BF16), pltpu.VMEM((2, NX, NZ, NY, BR, 128), BF16),
        pltpu.VMEM((2, NZ, NY, BR, 128), BF16), pltpu.VMEM((2, NX, NZ, BR, 128), BF16),
        pltpu.VMEM((2, 2, NZ, NY, BR, 128), BF16), pltpu.VMEM((2, 2, NX, NZ, BR, 128), BF16),
        pltpu.VMEM((2, NZ, NY, BR, 128), BF16), pltpu.VMEM((2, NX, NZ, BR, 128), BF16),
        pltpu.VMEM((2, 2, NZ, BR, 128), BF16),
        pltpu.VMEM((2, 2, 2, NZ, BR, 128), BF16),
        pltpu.VMEM((2, 2, BR, 128), BF16), pltpu.VMEM((2, 2, BR, 128), BF16),
        pltpu.VMEM((3, 4, width // 128, 128), F32),
        dma((6,)), dma((nchunk,)), dma((nchunk,)), dma((nchunk,)), dma((nchunk,)),
        dma((2, 2, 6)), dma((2, 2, 6)), dma((2, 4)), dma((2, 4)), dma((3,)), dma((3,)),
    ]
    outs = pl.pallas_call(
        functools.partial(kernel, factor),
        out_shape=(
            jax.ShapeDtypeStruct((width // 128, 128), F32),
            jax.ShapeDtypeStruct((BR, units), F32),
            jax.ShapeDtypeStruct((BR, units), F32),
        ),
        in_specs=[pl.BlockSpec(memory_space=pltpu.SMEM)] + [hbm] * 8,
        out_specs=(vmem, vmem, vmem),
        scratch_shapes=scratch,
        compiler_params=pltpu.CompilerParams(
            collective_id=0, has_side_effects=True, vmem_limit_bytes=60 * 1024 * 1024
        ),
    )(sample_ids, inputs, cotangent, stored, act_exp, grad_exp, gain, down_weight, up_weight)
    return (outs[0].reshape(1, width), outs[1][None], outs[2][None])


def solution(mesh):
    placed = (
        P(None, "dp", None, None),
        P(None, "dp", None, None),
        P(None, "dp", None, None),
        P(None, "dp"),
        P(None, None, "dp", None, None),
        P(None, None, "dp", None, None),
        P("section", None),
        P("section", None, None),
        P("section", None, None),
    )
    return jax.shard_map(
        local,
        mesh=mesh,
        in_specs=placed,
        out_specs=(P("section", None), P("section", "dp", None), P("section", "dp", None)),
        check_vma=False,
    )
```

```python
import functools
import math

import jax
import jax.numpy as jnp
from jax import lax
from jax.experimental import pallas as pl
from jax.experimental.pallas import tpu as pltpu
from jax.sharding import PartitionSpec as P

EPS = 1e-05
MESH = pl.DeviceIdType.MESH
F32 = jnp.float32
BF16 = jnp.bfloat16
C = 32
TW = 512
NX, NZ, NY = 4, 2, 4
BR = 208


def dot_nn(a, b):
    return jnp.dot(a, b, preferred_element_type=F32)


def dot_nt(a, b):
    return lax.dot_general(a, b, (((1,), (1,)), ((), ())), preferred_element_type=F32)


def dot_tn(a, b):
    return lax.dot_general(a, b, (((0,), (0,)), ((), ())), preferred_element_type=F32)


def kernel(
    factor,
    ids_ref, inputs, cotangent, stored, act_exp, grad_exp, gain, down, up,
    out_gain, out_down, out_up,
    x_st, dyb_st, xn_st, xout, dyout, down_v, up_v, stored_v, ascale, gscale,
    act_v, grad_v, gain_v, turn_v, pad_v, r_st, p_st, ybuf, gg, acc_v,
    xnq, dybq, dpq, hq, p1_0, p1_1, rel2, frl2, p2, q2, zrecv, qrecv, gx,
    load_sem, xin_sem, xs_sem, dy_sem, ds_sem, ex_send, ex_recv, rs_send, rs_recv,
    gs_send, gs_recv, z_send, z_recv, q_send, q_recv,
):
    tokens, width = x_st.shape
    nchunk = tokens // C
    seq = inputs.shape[2]
    per = seq // C
    ntile = width // TW
    s = lax.axis_index("section")
    dp = lax.axis_index("dp")
    xc = lax.div(dp, NZ * NY)
    zc = lax.rem(lax.div(dp, NY), NZ)
    yc = lax.rem(dp, NY)
    last = lax.axis_size("section") - 1

    def at_x(t):
        return t * (NZ * NY) + zc * NY + yc

    def at_y(t):
        return xc * (NZ * NY) + zc * NY + t

    def turned(z):
        return yc * (NZ * NY) + z * NY + xc

    zmate = xc * (NZ * NY) + (1 - zc) * NY + yc

    loads = [
        pltpu.make_async_copy(act_exp.at[jnp.minimum(s, last - 1)], act_v, load_sem.at[0]),
        pltpu.make_async_copy(gain, gain_v, load_sem.at[1]),
        pltpu.make_async_copy(down.at[0], down_v, load_sem.at[2]),
        pltpu.make_async_copy(up.at[0], up_v, load_sem.at[3]),
        pltpu.make_async_copy(stored.at[jnp.minimum(s, last - 1)], stored_v, load_sem.at[4]),
        pltpu.make_async_copy(grad_exp.at[jnp.maximum(s - 1, 0)], grad_v, load_sem.at[5]),
    ]
    loads[0].start()
    loads[1].start()

    def rows_of(c):
        return pl.ds(pl.multiple_of(c * C, C), C)

    def own_rows(source, stash, sem):
        for c in range(nchunk):
            slot = c // per
            pltpu.make_async_copy(
                source.at[slot // 2, slot % 2, pl.ds((c % per) * C, C)],
                stash.at[pl.ds(c * C, C)],
                sem.at[c],
            ).start()

    @pl.when(s == 0)
    def _():
        own_rows(inputs, x_st, xin_sem)

    for load in loads[2:]:
        load.start()

    @pl.when(s == last)
    def _():
        own_rows(cotangent, dyb_st, dy_sem)

    barrier = pltpu.get_barrier_semaphore()
    for t in range(1, NX):
        pl.semaphore_signal(
            barrier, inc=1, device_id={"dp": at_x(lax.rem(xc + t, NX))}, device_id_type=MESH
        )
        pl.semaphore_signal(
            barrier, inc=1, device_id={"dp": at_y(lax.rem(yc + t, NY))}, device_id_type=MESH
        )
    pl.semaphore_signal(barrier, inc=1, device_id={"dp": zmate}, device_id_type=MESH)

    @pl.when(xc != yc)
    def _():
        for z in range(NZ):
            pl.semaphore_signal(barrier, inc=1, device_id={"dp": turned(z)}, device_id_type=MESH)

    @pl.when(s > 0)
    def _():
        pl.semaphore_signal(barrier, inc=1, device_id={"section": s - 1}, device_id_type=MESH)

    @pl.when(s < last)
    def _():
        pl.semaphore_signal(barrier, inc=1, device_id={"section": s + 1}, device_id_type=MESH)

    def expand(exps, out):
        turn_v[...] = jnp.zeros_like(turn_v)
        for m in range(exps.shape[0]):
            for i in range(exps.shape[2]):
                own = exps[m, :, i, :]
                scale = jnp.left_shift(jnp.ones(own.shape, jnp.int32), own + 8).astype(F32) / 256.0
                at = (m * exps.shape[2] + i) * seq
                turn_v[: exps.shape[1], at : at + seq] = scale
        pad_v[...] = jnp.transpose(turn_v[...]).astype(BF16)

        def tile(k, carry):
            cols = pl.ds(pl.multiple_of(k * TW, TW), TW)
            block = lax.broadcasted_iota(jnp.int32, (pad_v.shape[1], TW), 0)
            lane = lax.broadcasted_iota(jnp.int32, (pad_v.shape[1], TW), 1)
            pick = (block == k * (TW // 128) + jnp.right_shift(lane, 7)).astype(F32).astype(BF16)
            out[:, cols] = dot_nn(pad_v[...], pick).astype(BF16)
            return carry

        lax.fori_loop(0, ntile, tile, 0)

    gg[...] = jnp.zeros_like(gg)
    loads[0].wait()
    loads[5].wait()

    @pl.when(s < last)
    def _():
        expand(act_v, ascale)

    @pl.when(s > 0)
    def _():
        expand(grad_v, gscale)

    for load in loads[1:5]:
        load.wait()

    npeer = NX - 1 + NY - 1 + 1
    npeer = npeer + jnp.where(xc != yc, NZ, 0)
    pl.semaphore_wait(barrier, npeer + jnp.where(s > 0, 1, 0) + jnp.where(s < last, 1, 0))

    def send_x(c):
        return pltpu.make_async_remote_copy(
            src_ref=xout.at[rows_of(c)], dst_ref=x_st.at[rows_of(c)],
            send_sem=xs_sem.at[c], recv_sem=xin_sem.at[c],
            device_id={"section": s + 1}, device_id_type=MESH,
        )

    def send_dy(c):
        return pltpu.make_async_remote_copy(
            src_ref=dyout.at[rows_of(c)], dst_ref=dyb_st.at[rows_of(c)],
            send_sem=ds_sem.at[c], recv_sem=dy_sem.at[c],
            device_id={"section": s - 1}, device_id_type=MESH,
        )

    quarter = width // 4

    def ring_x(t):
        return at_x(lax.rem(xc + t, 4)), lax.rem(xc + t, 4), xc

    def ring_y(t):
        return at_y(lax.rem(yc + t, 4)), lax.rem(yc + t, 4), yc

    def quarters(kind, t, stash, out, rows):
        to, other, mine = (ring_x, ring_y)[kind](t)
        cols = pl.ds(pl.multiple_of(other * quarter, 128), quarter)
        return pltpu.make_async_remote_copy(
            src_ref=stash.at[rows, cols], dst_ref=out.at[mine, rows],
            send_sem=ex_send.at[kind, 0, t], recv_sem=ex_recv.at[kind, 0, mine],
            device_id={"dp": to}, device_id_type=MESH,
        )

    def units_of(kind, t, out, rows):
        to, other, mine = (ring_x, ring_y)[kind](t)
        return pltpu.make_async_remote_copy(
            src_ref=out.at[mine, rows], dst_ref=out.at[mine, rows],
            send_sem=ex_send.at[kind, 1, t], recv_sem=ex_recv.at[kind, 1, mine],
            device_id={"dp": to}, device_id_type=MESH,
        )

    def own_quarter(kind, stash, out, rows):
        mine = (xc, yc)[kind]
        cols = pl.ds(pl.multiple_of(mine * quarter, 128), quarter)
        return pltpu.make_async_copy(
            stash.at[rows, cols], out.at[mine, rows], ex_recv.at[kind, 0, mine]
        )

    def exchange(kind, stash, out, rows):
        for t in (2, 1, 3):
            quarters(kind, t, stash, out, rows).start()
        own_quarter(kind, stash, out, rows).start()

    def exchange_units(kind, out, rows):
        for t in (2, 1, 3):
            units_of(kind, t, out, rows).start()

    def exchanged(kind, part, out):
        mine = (xc, yc)[kind]
        for t in range(1 if part else 0, 4):
            other = lax.rem(mine + t, 4)
            pltpu.make_async_copy(
                out.at[other], out.at[other], ex_recv.at[kind, part, other]
            ).wait()

    def cols_of(k):
        return pl.ds(pl.multiple_of(k * TW, TW), TW)

    def forward(c):
        rows = rows_of(c)
        pltpu.make_async_copy(x_st.at[rows], x_st.at[rows], xin_sem.at[c]).wait()

        def square(k, acc):
            x = x_st[rows, cols_of(k)].astype(F32)
            return acc + x * x

        acc = lax.fori_loop(0, ntile, square, jnp.zeros((C, TW), F32), unroll=True)
        recip = lax.rsqrt(jnp.sum(acc, axis=1, keepdims=True) / width + EPS)
        r_st[rows, :] = jnp.broadcast_to(recip, (C, 128))
        wide = jnp.broadcast_to(recip, (C, TW))

        def norm(k, carry):
            x = x_st[rows, cols_of(k)].astype(F32)
            xn_st[rows, cols_of(k)] = (x * wide * gain_v[:, cols_of(k)]).astype(BF16)
            return carry

        lax.fori_loop(0, ntile, norm, 0, unroll=True)
        pre = dot_nn(xn_st[rows, :], down_v[...])
        hidden = (pre * jax.nn.sigmoid(pre)).astype(BF16)
        p_st[rows, :] = pre
        hq[yc, rows, :] = hidden

        @pl.when(s < last)
        def _():
            ybuf[...] = dot_nt(hidden, up_v[...])
            slot = lax.div(c, per)
            pos = pl.ds(pl.multiple_of(lax.rem(c, per) * C, C), C)
            own = ids_ref[lax.div(slot, 2), lax.rem(slot, 2)] - dp * stored_v.shape[0]
            own = jnp.clip(own, 0, stored_v.shape[0] - 1)

            def code(k, carry):
                cols = cols_of(k)
                y = x_st[rows, cols].astype(F32) + ybuf[:, cols]
                base = stored_v[own, pos, cols].astype(F32)
                scale = ascale[rows, cols].astype(F32)
                step = jnp.clip(y - base, -8.0 * scale, 7.0 * scale)
                xout[rows, cols] = (base + step).astype(BF16)
                return carry

            lax.fori_loop(0, ntile, code, 0, unroll=True)
            send_x(c).start()

        exchange(0, xn_st, xnq, rows)
        exchange_units(1, hq, rows)

    def backward(c):
        rows = rows_of(c)
        pltpu.make_async_copy(dyb_st.at[rows], dyb_st.at[rows], dy_sem.at[c]).wait()
        dh = dot_nn(dyb_st[rows, :], up_v[...])
        pre = p_st[rows, :]
        sig = jax.nn.sigmoid(pre)
        dpre = (dh * sig * (1.0 + pre * (1.0 - sig))).astype(BF16)
        dpq[xc, rows, :] = dpre
        exchange(1, dyb_st, dybq, rows)
        exchange_units(0, dpq, rows)
        ybuf[...] = dot_nt(dpre, down_v[...])
        wide = jnp.concatenate([r_st[rows, :]] * (TW // 128), axis=1)

        def first(k, acc):
            cols = cols_of(k)
            prod = ybuf[:, cols] * (x_st[rows, cols].astype(F32) * wide)
            gg[:, cols] += jnp.sum(prod.reshape(C // 8, 8, TW), axis=0)
            return acc + prod * gain_v[:, cols]

        acc = lax.fori_loop(0, ntile, first, jnp.zeros((C, TW), F32), unroll=True)

        @pl.when(s > 0)
        def _():
            mean = jnp.broadcast_to(jnp.sum(acc, axis=1, keepdims=True) / width, (C, TW))

            def second(k, carry):
                cols = cols_of(k)
                z = x_st[rows, cols].astype(F32) * wide
                dz = ybuf[:, cols] * gain_v[:, cols]
                grad = wide * (dz - z * mean) + dyb_st[rows, cols].astype(F32)
                scale = gscale[rows, cols].astype(F32)
                dyout[rows, cols] = jnp.clip(grad, -128.0 * scale, 127.0 * scale).astype(BF16)
                return carry

            lax.fori_loop(0, ntile, second, 0, unroll=True)
            send_dy(c).start()

    lag = jnp.where(s == last, 0, jnp.where(s == last - 1, 2, nchunk))

    def step(t, carry):
        @pl.when(t < nchunk)
        def _():
            forward(t)

        @pl.when((t >= lag) & (t < lag + nchunk))
        def _():
            backward(t - lag)

        return carry

    lax.fori_loop(0, 2 * nchunk, step, 0)

    nrow = width // 128
    for b in range(nrow):
        gx[0, xc, b : b + 1, :] = jnp.sum(gg[:, b * 128 : (b + 1) * 128], axis=0, keepdims=True)

    def gain_send(phase, t):
        coord, at = ((xc, at_x), (yc, at_y))[phase]
        return pltpu.make_async_remote_copy(
            src_ref=gx.at[phase, coord], dst_ref=gx.at[phase, coord],
            send_sem=gs_send.at[phase, t], recv_sem=gs_recv.at[phase, coord],
            device_id={"dp": at(lax.rem(coord + t, 4))}, device_id_type=MESH,
        )

    def gain_wait(phase):
        coord = (xc, yc)[phase]
        for t in range(1, 4):
            other = lax.rem(coord + t, 4)
            pltpu.make_async_copy(
                gx.at[phase, other], gx.at[phase, other], gs_recv.at[phase, other]
            ).wait()

    def gain_sum(phase):
        return (gx[phase, 0] + gx[phase, 1]) + (gx[phase, 2] + gx[phase, 3])

    for t in range(1, 4):
        gain_send(0, t).start()

    def grads(data, units, out):
        def add_source(k, carry):
            value = dot_tn(data[k], units[k])

            @pl.when(k == 0)
            def _():
                acc_v[...] = value

            @pl.when(k > 0)
            def _():
                acc_v[...] += value

            return carry

        lax.fori_loop(0, 4, add_source, 0)
        for a in range(2):
            value = acc_v[:, a * 128 : (a + 1) * 128].astype(BF16)
            out[a] = value.reshape(NZ, NY, BR, 128)

    def ring_sends(kind, phase, chunk, rel, frl, coord, at):
        right, left, opp = lax.rem(coord + 1, 4), lax.rem(coord + 3, 4), lax.rem(coord + 2, 4)

        def copy(i, src, dst, to):
            return pltpu.make_async_remote_copy(
                src_ref=src, dst_ref=dst,
                send_sem=rs_send.at[kind, phase, i], recv_sem=rs_recv.at[kind, phase, i],
                device_id={"dp": at(to)}, device_id_type=MESH,
            )

        return [
            copy(0, chunk(0, opp), rel.at[0], right),
            copy(1, chunk(1, opp), rel.at[1], left),
            copy(2, chunk(1, right), frl.at[0, 1], right),
            copy(3, chunk(0, left), frl.at[1, 0], left),
            copy(4, chunk(0, right), frl.at[0, 0], right),
            copy(5, chunk(1, left), frl.at[1, 1], left),
        ]

    sends = [
        ring_sends(0, 0, lambda a, t: p1_0.at[a, :, t], rel2.at[0], frl2.at[0], yc, at_y),
        ring_sends(1, 0, lambda a, t: p1_1.at[a, :, t], rel2.at[1], frl2.at[1], xc, at_x),
    ]

    def add(*refs):
        total = refs[0][...].astype(F32)
        for ref in refs[1:]:
            total = total + ref[...].astype(F32)
        return total

    def loop(n, body):
        def run(i, carry):
            body(i)
            return carry

        lax.fori_loop(0, n, run, 0)

    rings = ((p1_0, yc), (p1_1, xc))

    def begin(kind, stash_q, units_q):
        exchanged(kind, 0, stash_q)
        exchanged(kind, 1, units_q)
        grads(stash_q, units_q, rings[kind][0])
        for i in range(4):
            sends[kind][i].start()

    def relay(kind):
        buf, coord = rings[kind]
        for a, to in ((0, lax.rem(coord + 1, 4)), (1, lax.rem(coord + 3, 4))):
            sends[kind][a].wait_recv()

            def body(v, a=a, to=to):
                buf[a, v, to] = add(buf.at[a, v, to], rel2.at[kind, a, v]).astype(BF16)

            loop(NZ, body)
            sends[kind][4 + a].start()

    begin(0, xnq, dpq)
    begin(1, dybq, hq)
    relay(0)
    relay(1)
    gain_wait(0)
    gx[1, yc] = gain_sum(0)
    for t in range(1, 4):
        gain_send(1, t).start()

    def mate(i, ref_src, ref_dst):
        return pltpu.make_async_remote_copy(
            src_ref=ref_src, dst_ref=ref_dst, send_sem=z_send.at[i], recv_sem=z_recv.at[i],
            device_id={"dp": zmate}, device_id_type=MESH,
        )

    def summed(kind, a, z):
        buf, coord = rings[kind]
        return add(buf.at[a, z, coord], frl2.at[kind, 0, a, z], frl2.at[kind, 1, a, z])

    for i in range(2, 6):
        sends[0][i].wait_recv()
    for a in range(2):
        p2[a] = summed(0, a, 1 - zc).astype(BF16)
    zdown = mate(0, p2, zrecv)
    zdown.start()

    def turn(z):
        return pltpu.make_async_remote_copy(
            src_ref=q2.at[z], dst_ref=qrecv.at[zc],
            send_sem=q_send.at[z], recv_sem=q_recv.at[zc],
            device_id={"dp": turned(z)}, device_id_type=MESH,
        )

    for i in range(2, 6):
        sends[1][i].wait_recv()
    for z in range(NZ):
        for a in range(2):
            q2[z, a] = summed(1, a, z).astype(BF16)

        @pl.when(turned(z) != dp)
        def _():
            turn(z).start()

        @pl.when(turned(z) == dp)
        def _():
            pltpu.make_async_copy(q2.at[z], qrecv.at[zc], q_recv.at[zc]).start()

    gain_wait(1)
    gx[2, zc] = gain_sum(1)
    zgain = mate(1, gx.at[2, zc], gx.at[2, zc])
    zgain.start()

    zdown.wait_recv()
    for a in range(2):
        out_down[:, a * 128 : (a + 1) * 128] = (
            summed(0, a, zc) + zrecv[a].astype(F32)
        ) * factor
    for z in range(NZ):
        pltpu.make_async_copy(qrecv.at[z], qrecv.at[z], q_recv.at[z]).wait()
    for a in range(2):
        out_up[:, a * 128 : (a + 1) * 128] = add(qrecv.at[0, a], qrecv.at[1, a]) * factor

    pltpu.make_async_copy(gx.at[2, 1 - zc], gx.at[2, 1 - zc], z_recv.at[1]).wait()
    out_gain[...] = (gx[2, 0] + gx[2, 1]) * factor

    zgain.wait_send()
    zdown.wait_send()
    for z in range(NZ):

        @pl.when(turned(z) != dp)
        def _():
            turn(z).wait_send()

    for kind in (0, 1):
        for i in range(6):
            sends[kind][i].wait_send()
    every = pl.ds(0, tokens)
    for t in range(1, 4):
        quarters(0, t, xn_st, xnq, every).wait_send()
        quarters(1, t, dyb_st, dybq, every).wait_send()
        units_of(0, t, dpq, every).wait_send()
        units_of(1, t, hq, every).wait_send()
    for phase in (0, 1):
        for t in range(1, 4):
            gain_send(phase, t).wait_send()

    @pl.when(s < last)
    def _():
        loop(nchunk, lambda c: send_x(c).wait_send())

    @pl.when(s > 0)
    def _():
        loop(nchunk, lambda c: send_dy(c).wait_send())


def local(inputs, cotangent, stored, sample_ids, act_exp, grad_exp, gain, down_weight, up_weight):
    micro, spm, seq, width = inputs.shape
    tokens = micro * spm * seq
    units = down_weight.shape[2]
    act_exp = jnp.transpose(act_exp, (0, 1, 4, 2, 3))
    grad_exp = jnp.transpose(grad_exp, (0, 1, 4, 2, 3))
    nchunk = tokens // C
    ndp = lax.axis_size("dp")
    factor = 1.0 / math.sqrt(tokens * ndp)
    hbm = pl.BlockSpec(memory_space=pl.ANY)
    vmem = pl.BlockSpec(memory_space=pltpu.VMEM)
    big = pltpu.VMEM((tokens, width), BF16)
    dma = pltpu.SemaphoreType.DMA
    scratch = [
        big, big, big, big, big,
        pltpu.VMEM((width, units), BF16), pltpu.VMEM((width, units), BF16),
        pltpu.VMEM(stored.shape[1:], BF16),
        big, big,
        pltpu.VMEM(act_exp.shape[1:], jnp.int32), pltpu.VMEM(grad_exp.shape[1:], jnp.int32),
        pltpu.VMEM((1, width), F32),
        pltpu.VMEM((128, tokens), F32),
        pltpu.VMEM((tokens, 128), BF16),
        pltpu.VMEM((tokens, 128), F32),
        pltpu.VMEM((tokens, units), F32),
        pltpu.VMEM((C, width), F32),
        pltpu.VMEM((8, width), F32),
        pltpu.VMEM((width // 4, units), F32),
        pltpu.VMEM((4, tokens, width // 4), BF16), pltpu.VMEM((4, tokens, width // 4), BF16),
        pltpu.VMEM((4, tokens, units), BF16), pltpu.VMEM((4, tokens, units), BF16),
        pltpu.VMEM((2, NZ, NY, BR, 128), BF16), pltpu.VMEM((2, NZ, NY, BR, 128), BF16),
        pltpu.VMEM((2, 2, NZ, BR, 128), BF16),
        pltpu.VMEM((2, 2, 2, NZ, BR, 128), BF16),
        pltpu.VMEM((2, BR, 128), BF16), pltpu.VMEM((2, 2, BR, 128), BF16),
        pltpu.VMEM((2, BR, 128), BF16), pltpu.VMEM((2, 2, BR, 128), BF16),
        pltpu.VMEM((3, 4, width // 128, 128), F32),
        dma((6,)), dma((nchunk,)), dma((nchunk,)), dma((nchunk,)), dma((nchunk,)),
        dma((2, 2, 4)), dma((2, 2, 4)), dma((2, 1, 6)), dma((2, 1, 6)),
        dma((2, 4)), dma((2, 4)), dma((2,)), dma((2,)), dma((2,)), dma((2,)),
    ]
    outs = pl.pallas_call(
        functools.partial(kernel, factor),
        out_shape=(
            jax.ShapeDtypeStruct((width // 128, 128), F32),
            jax.ShapeDtypeStruct((BR, units), F32),
            jax.ShapeDtypeStruct((BR, units), F32),
        ),
        in_specs=[pl.BlockSpec(memory_space=pltpu.SMEM)] + [hbm] * 8,
        out_specs=(vmem, vmem, vmem),
        scratch_shapes=scratch,
        compiler_params=pltpu.CompilerParams(
            collective_id=0, has_side_effects=True, vmem_limit_bytes=60 * 1024 * 1024
        ),
    )(sample_ids, inputs, cotangent, stored, act_exp, grad_exp, gain, down_weight, up_weight)
    return (outs[0].reshape(1, width), outs[1][None], outs[2][None])


def solution(mesh):
    placed = (
        P(None, "dp", None, None),
        P(None, "dp", None, None),
        P(None, "dp", None, None),
        P(None, "dp"),
        P(None, None, "dp", None, None),
        P(None, None, "dp", None, None),
        P("section", None),
        P("section", None, None),
        P("section", None, None),
    )
    return jax.shard_map(
        local,
        mesh=mesh,
        in_specs=placed,
        out_specs=(P("section", None), P("section", "dp", None), P("section", "dp", None)),
        check_vma=False,
    )
```

```python
import functools
import math

import jax
import jax.numpy as jnp
from jax import lax
from jax.experimental import pallas as pl
from jax.experimental.pallas import tpu as pltpu
from jax.sharding import PartitionSpec as P

EPS = 1e-05
MESH = pl.DeviceIdType.MESH
F32 = jnp.float32
BF16 = jnp.bfloat16
C = 32
TW = 512
NX, NZ, NY = 4, 2, 4
BR = 208


def dot_nn(a, b):
    return jnp.dot(a, b, preferred_element_type=F32)


def dot_nt(a, b):
    return lax.dot_general(a, b, (((1,), (1,)), ((), ())), preferred_element_type=F32)


def dot_tn(a, b):
    return lax.dot_general(a, b, (((0,), (0,)), ((), ())), preferred_element_type=F32)


def kernel(
    factor,
    ids_ref, inputs, cotangent, stored, act_exp, grad_exp, gain, down, up,
    out_gain, out_down, out_up,
    x_st, dyb_st, xn_st, xout, dyout, down_v, up_v, stored_v, ascale, gscale,
    act_v, grad_v, gain_v, turn_v, pad_v, r_st, p_st, ybuf, gg, acc_v,
    xnq, dybq, dpq, hq, p1_0, p1_1, rel2, frl2, q2, qrecv, gx,
    load_sem, xin_sem, xs_sem, dy_sem, ds_sem, ex_send, ex_recv, rs_send, rs_recv,
    gs_send, gs_recv, z_send, z_recv, q_send, q_recv,
):
    tokens, width = x_st.shape
    nchunk = tokens // C
    seq = inputs.shape[2]
    per = seq // C
    ntile = width // TW
    s = lax.axis_index("section")
    dp = lax.axis_index("dp")
    xc = lax.div(dp, NZ * NY)
    zc = lax.rem(lax.div(dp, NY), NZ)
    yc = lax.rem(dp, NY)
    last = lax.axis_size("section") - 1

    def at_x(t):
        return t * (NZ * NY) + zc * NY + yc

    def at_y(t):
        return xc * (NZ * NY) + zc * NY + t

    by_x = [s >= 0, lax.rem(s, 2) == 0]
    mine = [jnp.where(by_x[kind], xc, yc) for kind in (0, 1)]
    cross = [jnp.where(by_x[kind], yc, xc) for kind in (0, 1)]

    def ring_id(kind, t):
        return jnp.where(by_x[kind], at_x(t), at_y(t))

    def cross_id(kind, t):
        return jnp.where(by_x[kind], at_y(t), at_x(t))

    def owner(kind, z):
        return mine[kind] * (NZ * NY) + z * NY + cross[kind]

    def turned(z):
        return yc * (NZ * NY) + z * NY + xc

    zmate = xc * (NZ * NY) + (1 - zc) * NY + yc

    loads = [
        pltpu.make_async_copy(act_exp.at[jnp.minimum(s, last - 1)], act_v, load_sem.at[0]),
        pltpu.make_async_copy(gain, gain_v, load_sem.at[1]),
        pltpu.make_async_copy(down.at[0], down_v, load_sem.at[2]),
        pltpu.make_async_copy(up.at[0], up_v, load_sem.at[3]),
        pltpu.make_async_copy(stored.at[jnp.minimum(s, last - 1)], stored_v, load_sem.at[4]),
        pltpu.make_async_copy(grad_exp.at[jnp.maximum(s - 1, 0)], grad_v, load_sem.at[5]),
    ]
    loads[0].start()
    loads[1].start()

    def rows_of(c):
        return pl.ds(pl.multiple_of(c * C, C), C)

    def own_rows(source, stash, sem, first, end):
        for c in range(first, end):
            slot = c // per
            pltpu.make_async_copy(
                source.at[slot // 2, slot % 2, pl.ds((c % per) * C, C)],
                stash.at[pl.ds(c * C, C)],
                sem.at[c],
            ).start()

    @pl.when(s == 0)
    def _():
        own_rows(inputs, x_st, xin_sem, 0, 1)

    for load in loads[2:]:
        load.start()

    @pl.when(s == 0)
    def _():
        own_rows(inputs, x_st, xin_sem, 1, nchunk)

    @pl.when(s == last)
    def _():
        own_rows(cotangent, dyb_st, dy_sem, 0, nchunk)

    barrier = pltpu.get_barrier_semaphore()
    for t in range(1, NX):
        pl.semaphore_signal(
            barrier, inc=1, device_id={"dp": at_x(lax.rem(xc + t, NX))}, device_id_type=MESH
        )
        pl.semaphore_signal(
            barrier, inc=1, device_id={"dp": at_y(lax.rem(yc + t, NY))}, device_id_type=MESH
        )
    pl.semaphore_signal(barrier, inc=1, device_id={"dp": zmate}, device_id_type=MESH)

    @pl.when(xc != yc)
    def _():
        for z in range(NZ):
            pl.semaphore_signal(barrier, inc=1, device_id={"dp": turned(z)}, device_id_type=MESH)

    @pl.when(s > 0)
    def _():
        pl.semaphore_signal(barrier, inc=1, device_id={"section": s - 1}, device_id_type=MESH)

    @pl.when(s < last)
    def _():
        pl.semaphore_signal(barrier, inc=1, device_id={"section": s + 1}, device_id_type=MESH)

    def expand(exps, out):
        turn_v[...] = jnp.zeros_like(turn_v)
        for m in range(exps.shape[0]):
            for i in range(exps.shape[2]):
                own = exps[m, :, i, :]
                scale = jnp.left_shift(jnp.ones(own.shape, jnp.int32), own + 8).astype(F32) / 256.0
                at = (m * exps.shape[2] + i) * seq
                turn_v[: exps.shape[1], at : at + seq] = scale
        pad_v[...] = jnp.transpose(turn_v[...]).astype(BF16)

        def tile(k, carry):
            cols = pl.ds(pl.multiple_of(k * TW, TW), TW)
            block = lax.broadcasted_iota(jnp.int32, (pad_v.shape[1], TW), 0)
            lane = lax.broadcasted_iota(jnp.int32, (pad_v.shape[1], TW), 1)
            pick = (block == k * (TW // 128) + jnp.right_shift(lane, 7)).astype(F32).astype(BF16)
            out[:, cols] = dot_nn(pad_v[...], pick).astype(BF16)
            return carry

        lax.fori_loop(0, ntile, tile, 0)

    gg[...] = jnp.zeros_like(gg)
    loads[0].wait()

    @pl.when(s < last)
    def _():
        expand(act_v, ascale)

    loads[5].wait()

    @pl.when(s > 0)
    def _():
        expand(grad_v, gscale)

    loads[1].wait()

    npeer = NX - 1 + NY - 1 + 1
    npeer = npeer + jnp.where(xc != yc, NZ, 0)
    pl.semaphore_wait(barrier, npeer + jnp.where(s > 0, 1, 0) + jnp.where(s < last, 1, 0))

    def send_x(c):
        return pltpu.make_async_remote_copy(
            src_ref=xout.at[rows_of(c)], dst_ref=x_st.at[rows_of(c)],
            send_sem=xs_sem.at[c], recv_sem=xin_sem.at[c],
            device_id={"section": s + 1}, device_id_type=MESH,
        )

    def send_dy(c):
        return pltpu.make_async_remote_copy(
            src_ref=dyout.at[rows_of(c)], dst_ref=dyb_st.at[rows_of(c)],
            send_sem=ds_sem.at[c], recv_sem=dy_sem.at[c],
            device_id={"section": s - 1}, device_id_type=MESH,
        )

    quarter = width // 4

    def quarters(kind, t, stash, out, rows):
        other = lax.rem(mine[kind] + t, 4)
        cols = pl.ds(pl.multiple_of(other * quarter, 128), quarter)
        return pltpu.make_async_remote_copy(
            src_ref=stash.at[rows, cols], dst_ref=out.at[mine[kind], rows],
            send_sem=ex_send.at[kind, 0, t], recv_sem=ex_recv.at[kind, 0, mine[kind]],
            device_id={"dp": ring_id(kind, other)}, device_id_type=MESH,
        )

    def units_of(kind, t, out, rows):
        other = lax.rem(mine[kind] + t, 4)
        return pltpu.make_async_remote_copy(
            src_ref=out.at[mine[kind], rows], dst_ref=out.at[mine[kind], rows],
            send_sem=ex_send.at[kind, 1, t], recv_sem=ex_recv.at[kind, 1, mine[kind]],
            device_id={"dp": ring_id(kind, other)}, device_id_type=MESH,
        )

    def own_quarter(kind, stash, out, rows):
        cols = pl.ds(pl.multiple_of(mine[kind] * quarter, 128), quarter)
        return pltpu.make_async_copy(
            stash.at[rows, cols], out.at[mine[kind], rows], ex_recv.at[kind, 0, mine[kind]]
        )

    def exchange(kind, stash, out, rows):
        for t in (2, 1, 3):
            quarters(kind, t, stash, out, rows).start()
        own_quarter(kind, stash, out, rows).start()

    def exchange_units(kind, out, rows):
        for t in (2, 1, 3):
            units_of(kind, t, out, rows).start()

    def exchanged(kind, part, out):
        for t in range(1 if part else 0, 4):
            other = lax.rem(mine[kind] + t, 4)
            pltpu.make_async_copy(
                out.at[other], out.at[other], ex_recv.at[kind, part, other]
            ).wait()

    def cols_of(k):
        return pl.ds(pl.multiple_of(k * TW, TW), TW)

    def forward(c):
        rows = rows_of(c)
        pltpu.make_async_copy(x_st.at[rows], x_st.at[rows], xin_sem.at[c]).wait()

        def square(k, acc):
            x = x_st[rows, cols_of(k)].astype(F32)
            return acc + x * x

        acc = lax.fori_loop(0, ntile, square, jnp.zeros((C, TW), F32), unroll=True)
        recip = lax.rsqrt(jnp.sum(acc, axis=1, keepdims=True) / width + EPS)
        r_st[rows, :] = jnp.broadcast_to(recip, (C, 128))
        wide = jnp.broadcast_to(recip, (C, TW))

        def norm(k, carry):
            x = x_st[rows, cols_of(k)].astype(F32)
            xn_st[rows, cols_of(k)] = (x * wide * gain_v[:, cols_of(k)]).astype(BF16)
            return carry

        lax.fori_loop(0, ntile, norm, 0, unroll=True)

        @pl.when(c == 0)
        def _():
            loads[2].wait()

        pre = dot_nn(xn_st[rows, :], down_v[...])
        hidden = (pre * jax.nn.sigmoid(pre)).astype(BF16)
        p_st[rows, :] = pre
        hq[mine[1], rows, :] = hidden

        @pl.when(c == 0)
        def _():
            loads[3].wait()
            loads[4].wait()

        @pl.when(s < last)
        def _():
            ybuf[...] = dot_nt(hidden, up_v[...])
            slot = lax.div(c, per)
            pos = pl.ds(pl.multiple_of(lax.rem(c, per) * C, C), C)
            own = ids_ref[lax.div(slot, 2), lax.rem(slot, 2)] - dp * stored_v.shape[0]
            own = jnp.clip(own, 0, stored_v.shape[0] - 1)

            def code(k, carry):
                cols = cols_of(k)
                y = x_st[rows, cols].astype(F32) + ybuf[:, cols]
                base = stored_v[own, pos, cols].astype(F32)
                scale = ascale[rows, cols].astype(F32)
                step = jnp.clip(y - base, -8.0 * scale, 7.0 * scale)
                xout[rows, cols] = (base + step).astype(BF16)
                return carry

            lax.fori_loop(0, ntile, code, 0, unroll=True)
            send_x(c).start()

        exchange(0, xn_st, xnq, rows)
        exchange_units(1, hq, rows)

    def backward(c):
        rows = rows_of(c)
        pltpu.make_async_copy(dyb_st.at[rows], dyb_st.at[rows], dy_sem.at[c]).wait()

        @pl.when(s == 0)
        def _():
            exchange(1, dyb_st, dybq, rows)

        dh = dot_nn(dyb_st[rows, :], up_v[...])
        pre = p_st[rows, :]
        sig = jax.nn.sigmoid(pre)
        dpre = (dh * sig * (1.0 + pre * (1.0 - sig))).astype(BF16)
        dpq[mine[0], rows, :] = dpre
        exchange_units(0, dpq, rows)
        ybuf[...] = dot_nt(dpre, down_v[...])
        wide = jnp.concatenate([r_st[rows, :]] * (TW // 128), axis=1)

        def first(k, acc):
            cols = cols_of(k)
            prod = ybuf[:, cols] * (x_st[rows, cols].astype(F32) * wide)
            gg[:, cols] += jnp.sum(prod.reshape(C // 8, 8, TW), axis=0)
            return acc + prod * gain_v[:, cols]

        acc = lax.fori_loop(0, ntile, first, jnp.zeros((C, TW), F32), unroll=True)

        @pl.when(s > 0)
        def _():
            mean = jnp.broadcast_to(jnp.sum(acc, axis=1, keepdims=True) / width, (C, TW))

            def second(k, carry):
                cols = cols_of(k)
                z = x_st[rows, cols].astype(F32) * wide
                dz = ybuf[:, cols] * gain_v[:, cols]
                grad = wide * (dz - z * mean) + dyb_st[rows, cols].astype(F32)
                scale = gscale[rows, cols].astype(F32)
                dyout[rows, cols] = jnp.clip(grad, -128.0 * scale, 127.0 * scale).astype(BF16)
                return carry

            lax.fori_loop(0, ntile, second, 0, unroll=True)
            send_dy(c).start()
            exchange(1, dyb_st, dybq, rows)

    lag = jnp.where(s == last, 0, jnp.where(s == last - 1, 2, nchunk))

    def step(t, carry):
        @pl.when(t < nchunk)
        def _():
            forward(t)

        @pl.when((t >= lag) & (t < lag + nchunk))
        def _():
            backward(t - lag)

        return carry

    lax.fori_loop(0, 2 * nchunk, step, 0)

    nrow = width // 128
    for b in range(nrow):
        gx[0, xc, b : b + 1, :] = jnp.sum(gg[:, b * 128 : (b + 1) * 128], axis=0, keepdims=True)

    def gain_send(phase, t):
        coord, at = ((xc, at_x), (yc, at_y))[phase]
        return pltpu.make_async_remote_copy(
            src_ref=gx.at[phase, coord], dst_ref=gx.at[phase, coord],
            send_sem=gs_send.at[phase, t], recv_sem=gs_recv.at[phase, coord],
            device_id={"dp": at(lax.rem(coord + t, 4))}, device_id_type=MESH,
        )

    def gain_wait(phase):
        coord = (xc, yc)[phase]
        for t in range(1, 4):
            other = lax.rem(coord + t, 4)
            pltpu.make_async_copy(
                gx.at[phase, other], gx.at[phase, other], gs_recv.at[phase, other]
            ).wait()

    def gain_sum(phase):
        return (gx[phase, 0] + gx[phase, 1]) + (gx[phase, 2] + gx[phase, 3])

    for t in range(1, 4):
        gain_send(0, t).start()

    def grads(data, units, out):
        def add_source(k, carry):
            value = dot_tn(data[k], units[k])

            @pl.when(k == 0)
            def _():
                acc_v[...] = value

            @pl.when(k > 0)
            def _():
                acc_v[...] += value

            return carry

        lax.fori_loop(0, 4, add_source, 0)
        for a in range(2):
            value = acc_v[:, a * 128 : (a + 1) * 128].astype(BF16)
            out[a] = value.reshape(NZ, NY, BR, 128)

    def ring_sends(kind, chunk, rel, frl):
        coord = cross[kind]
        right, left, opp = lax.rem(coord + 1, 4), lax.rem(coord + 3, 4), lax.rem(coord + 2, 4)

        def copy(i, src, dst, to):
            return pltpu.make_async_remote_copy(
                src_ref=src, dst_ref=dst,
                send_sem=rs_send.at[kind, i], recv_sem=rs_recv.at[kind, i],
                device_id={"dp": cross_id(kind, to)}, device_id_type=MESH,
            )

        return [
            copy(0, chunk(0, opp), rel.at[0], right),
            copy(1, chunk(1, opp), rel.at[1], left),
            copy(2, chunk(1, right), frl.at[0, 1], right),
            copy(3, chunk(0, left), frl.at[1, 0], left),
            copy(4, chunk(0, right), frl.at[0, 0], right),
            copy(5, chunk(1, left), frl.at[1, 1], left),
        ]

    sends = [
        ring_sends(0, lambda a, t: p1_0.at[a, :, t], rel2.at[0], frl2.at[0]),
        ring_sends(1, lambda a, t: p1_1.at[a, :, t], rel2.at[1], frl2.at[1]),
    ]

    def add(*refs):
        total = refs[0][...].astype(F32)
        for ref in refs[1:]:
            total = total + ref[...].astype(F32)
        return total

    def loop(n, body):
        def run(i, carry):
            body(i)
            return carry

        lax.fori_loop(0, n, run, 0)

    rings = ((p1_0, cross[0]), (p1_1, cross[1]))

    def begin(kind, stash_q, units_q):
        exchanged(kind, 0, stash_q)
        exchanged(kind, 1, units_q)
        grads(stash_q, units_q, rings[kind][0])
        for i in range(4):
            sends[kind][i].start()

    def relay(kind):
        buf, coord = rings[kind]
        for a, to in ((0, lax.rem(coord + 1, 4)), (1, lax.rem(coord + 3, 4))):
            sends[kind][a].wait_recv()

            def body(v, a=a, to=to):
                buf[a, v, to] = add(buf.at[a, v, to], rel2.at[kind, a, v]).astype(BF16)

            loop(NZ, body)
            sends[kind][4 + a].start()

    def turn(kind, z):
        return pltpu.make_async_remote_copy(
            src_ref=q2.at[kind, z], dst_ref=qrecv.at[kind, zc],
            send_sem=q_send.at[kind, z], recv_sem=q_recv.at[kind, zc],
            device_id={"dp": owner(kind, z)}, device_id_type=MESH,
        )

    def finish(kind):
        buf, coord = rings[kind]
        for i in range(2, 6):
            sends[kind][i].wait_recv()
        for z in range(NZ):
            for a in range(2):
                q2[kind, z, a] = add(
                    buf.at[a, z, coord], frl2.at[kind, 0, a, z], frl2.at[kind, 1, a, z]
                ).astype(BF16)

            @pl.when(owner(kind, z) != dp)
            def _():
                turn(kind, z).start()

            @pl.when(owner(kind, z) == dp)
            def _():
                pltpu.make_async_copy(
                    q2.at[kind, z], qrecv.at[kind, zc], q_recv.at[kind, zc]
                ).start()

    begin(0, xnq, dpq)
    gain_wait(0)
    gx[1, yc] = gain_sum(0)
    for t in range(1, 4):
        gain_send(1, t).start()
    begin(1, dybq, hq)
    relay(0)
    relay(1)
    finish(0)
    gain_wait(1)
    gx[2, zc] = gain_sum(1)
    zgain = pltpu.make_async_remote_copy(
        src_ref=gx.at[2, zc], dst_ref=gx.at[2, zc], send_sem=z_send.at[0], recv_sem=z_recv.at[0],
        device_id={"dp": zmate}, device_id_type=MESH,
    )
    zgain.start()
    finish(1)
    for kind, out in ((0, out_down), (1, out_up)):
        for z in range(NZ):
            pltpu.make_async_copy(
                qrecv.at[kind, z], qrecv.at[kind, z], q_recv.at[kind, z]
            ).wait()
        for a in range(2):
            out[:, a * 128 : (a + 1) * 128] = (
                add(qrecv.at[kind, 0, a], qrecv.at[kind, 1, a]) * factor
            )
    pltpu.make_async_copy(gx.at[2, 1 - zc], gx.at[2, 1 - zc], z_recv.at[0]).wait()
    out_gain[...] = (gx[2, 0] + gx[2, 1]) * factor

    zgain.wait_send()
    for kind in (0, 1):
        for z in range(NZ):

            @pl.when(owner(kind, z) != dp)
            def _():
                turn(kind, z).wait_send()

        for i in range(6):
            sends[kind][i].wait_send()
    every = pl.ds(0, tokens)
    for t in range(1, 4):
        quarters(0, t, xn_st, xnq, every).wait_send()
        quarters(1, t, dyb_st, dybq, every).wait_send()
        units_of(0, t, dpq, every).wait_send()
        units_of(1, t, hq, every).wait_send()
    for phase in (0, 1):
        for t in range(1, 4):
            gain_send(phase, t).wait_send()

    @pl.when(s < last)
    def _():
        loop(nchunk, lambda c: send_x(c).wait_send())

    @pl.when(s > 0)
    def _():
        loop(nchunk, lambda c: send_dy(c).wait_send())


def results(gain_ref, down_ref, up_ref, out_gain, out_down, out_up):
    for b in range(gain_ref.shape[0]):
        out_gain[:, b * 128 : (b + 1) * 128] = gain_ref[b : b + 1, :]
    out_down[0] = down_ref[...]
    out_up[0] = up_ref[...]


def local(inputs, cotangent, stored, sample_ids, act_exp, grad_exp, gain, down_weight, up_weight):
    micro, spm, seq, width = inputs.shape
    tokens = micro * spm * seq
    units = down_weight.shape[2]
    act_exp = jnp.transpose(act_exp, (0, 1, 4, 2, 3))
    grad_exp = jnp.transpose(grad_exp, (0, 1, 4, 2, 3))
    nchunk = tokens // C
    ndp = lax.axis_size("dp")
    factor = 1.0 / math.sqrt(tokens * ndp)
    hbm = pl.BlockSpec(memory_space=pl.ANY)
    vmem = pl.BlockSpec(memory_space=pltpu.VMEM)
    big = pltpu.VMEM((tokens, width), BF16)
    dma = pltpu.SemaphoreType.DMA
    scratch = [
        big, big, big, big, big,
        pltpu.VMEM((width, units), BF16), pltpu.VMEM((width, units), BF16),
        pltpu.VMEM(stored.shape[1:], BF16),
        big, big,
        pltpu.VMEM(act_exp.shape[1:], jnp.int32), pltpu.VMEM(grad_exp.shape[1:], jnp.int32),
        pltpu.VMEM((1, width), F32),
        pltpu.VMEM((128, tokens), F32),
        pltpu.VMEM((tokens, 128), BF16),
        pltpu.VMEM((tokens, 128), F32),
        pltpu.VMEM((tokens, units), F32),
        pltpu.VMEM((C, width), F32),
        pltpu.VMEM((8, width), F32),
        pltpu.VMEM((width // 4, units), F32),
        pltpu.VMEM((4, tokens, width // 4), BF16), pltpu.VMEM((4, tokens, width // 4), BF16),
        pltpu.VMEM((4, tokens, units), BF16), pltpu.VMEM((4, tokens, units), BF16),
        pltpu.VMEM((2, NZ, NY, BR, 128), BF16), pltpu.VMEM((2, NZ, NY, BR, 128), BF16),
        pltpu.VMEM((2, 2, NZ, BR, 128), BF16),
        pltpu.VMEM((2, 2, 2, NZ, BR, 128), BF16),
        pltpu.VMEM((2, 2, 2, BR, 128), BF16), pltpu.VMEM((2, 2, 2, BR, 128), BF16),
        pltpu.VMEM((3, 4, width // 128, 128), F32),
        dma((6,)), dma((nchunk,)), dma((nchunk,)), dma((nchunk,)), dma((nchunk,)),
        dma((2, 2, 4)), dma((2, 2, 4)), dma((2, 6)), dma((2, 6)),
        dma((2, 4)), dma((2, 4)), dma((1,)), dma((1,)), dma((2, 2)), dma((2, 2)),
    ]
    outs = pl.pallas_call(
        functools.partial(kernel, factor),
        out_shape=(
            jax.ShapeDtypeStruct((width // 128, 128), F32),
            jax.ShapeDtypeStruct((BR, units), F32),
            jax.ShapeDtypeStruct((BR, units), F32),
        ),
        in_specs=[pl.BlockSpec(memory_space=pltpu.SMEM)] + [hbm] * 8,
        out_specs=(vmem, vmem, vmem),
        scratch_shapes=scratch,
        compiler_params=pltpu.CompilerParams(
            collective_id=0, has_side_effects=True, vmem_limit_bytes=60 * 1024 * 1024
        ),
    )(sample_ids, inputs, cotangent, stored, act_exp, grad_exp, gain, down_weight, up_weight)
    return pl.pallas_call(
        results,
        out_shape=(
            jax.ShapeDtypeStruct((1, width), F32),
            jax.ShapeDtypeStruct((1, BR, units), F32),
            jax.ShapeDtypeStruct((1, BR, units), F32),
        ),
        in_specs=[vmem] * 3,
        out_specs=(vmem, vmem, vmem),
    )(*outs)


def solution(mesh):
    placed = (
        P(None, "dp", None, None),
        P(None, "dp", None, None),
        P(None, "dp", None, None),
        P(None, "dp"),
        P(None, None, "dp", None, None),
        P(None, None, "dp", None, None),
        P("section", None),
        P("section", None, None),
        P("section", None, None),
    )
    return jax.shard_map(
        local,
        mesh=mesh,
        in_specs=placed,
        out_specs=(P("section", None), P("section", "dp", None), P("section", "dp", None)),
        check_vma=False,
    )
```

```python
import functools
import math

import jax
import jax.numpy as jnp
from jax import lax
from jax.experimental import pallas as pl
from jax.experimental.pallas import tpu as pltpu
from jax.sharding import PartitionSpec as P

EPS = 1e-05
MESH = pl.DeviceIdType.MESH
F32 = jnp.float32
BF16 = jnp.bfloat16
C = 32
TW = 512
NX, NZ, NY = 4, 2, 4
BR = 208


def dot_nn(a, b):
    return jnp.dot(a, b, preferred_element_type=F32)


def dot_tn(a, b):
    return lax.dot_general(a, b, (((0,), (0,)), ((), ())), preferred_element_type=F32)


def kernel(
    factor,
    ids_ref, inputs, cotangent, stored, act_exp, grad_exp, gain, down, up,
    out_gain, out_down, out_up,
    x_st, dyb_st, xn_st, xout, dyout, down_v, up_v, stored_v, ascale, gscale,
    act_v, grad_v, gain_v, turn_v, pad_v, r_st, p_st, ybuf, gg, acc_v, up_t, down_t,
    xnq, dybq, dpq, hq, p1_0, p1_1, rel2, frl2, q2, qrecv, gx,
    load_sem, xin_sem, xs_sem, dy_sem, ds_sem, ex_send, ex_recv, rs_send, rs_recv,
    gs_send, gs_recv, z_send, z_recv, q_send, q_recv,
):
    tokens, width = x_st.shape
    nchunk = tokens // C
    seq = inputs.shape[2]
    per = seq // C
    ntile = width // TW
    s = lax.axis_index("section")
    dp = lax.axis_index("dp")
    xc = lax.div(dp, NZ * NY)
    zc = lax.rem(lax.div(dp, NY), NZ)
    yc = lax.rem(dp, NY)
    last = lax.axis_size("section") - 1

    def at_x(t):
        return t * (NZ * NY) + zc * NY + yc

    def at_y(t):
        return xc * (NZ * NY) + zc * NY + t

    by_x = [s != last - 1, lax.rem(s, 2) == 0]
    mine = [jnp.where(by_x[kind], xc, yc) for kind in (0, 1)]
    cross = [jnp.where(by_x[kind], yc, xc) for kind in (0, 1)]

    def ring_id(kind, t):
        return jnp.where(by_x[kind], at_x(t), at_y(t))

    def cross_id(kind, t):
        return jnp.where(by_x[kind], at_y(t), at_x(t))

    def owner(kind, z):
        return mine[kind] * (NZ * NY) + z * NY + cross[kind]

    def turned(z):
        return yc * (NZ * NY) + z * NY + xc

    zmate = xc * (NZ * NY) + (1 - zc) * NY + yc

    loads = [
        pltpu.make_async_copy(act_exp.at[jnp.minimum(s, last - 1)], act_v, load_sem.at[0]),
        pltpu.make_async_copy(gain, gain_v, load_sem.at[1]),
        pltpu.make_async_copy(up.at[0], up_v, load_sem.at[2]),
        pltpu.make_async_copy(down.at[0], down_v, load_sem.at[3]),
        pltpu.make_async_copy(stored.at[jnp.minimum(s, last - 1)], stored_v, load_sem.at[4]),
        pltpu.make_async_copy(grad_exp.at[jnp.maximum(s - 1, 0)], grad_v, load_sem.at[5]),
    ]
    loads[0].start()
    loads[1].start()

    def rows_of(c):
        return pl.ds(pl.multiple_of(c * C, C), C)

    def own_rows(source, stash, sem, first, end):
        for c in range(first, end):
            slot = c // per
            pltpu.make_async_copy(
                source.at[slot // 2, slot % 2, pl.ds((c % per) * C, C)],
                stash.at[pl.ds(c * C, C)],
                sem.at[c],
            ).start()

    @pl.when(s == 0)
    def _():
        own_rows(inputs, x_st, xin_sem, 0, 1)

    for load in loads[2:]:
        load.start()

    @pl.when(s == 0)
    def _():
        own_rows(inputs, x_st, xin_sem, 1, nchunk)

    @pl.when(s == last)
    def _():
        own_rows(cotangent, dyb_st, dy_sem, 0, nchunk)

    barrier = pltpu.get_barrier_semaphore()
    for t in range(1, NX):
        pl.semaphore_signal(
            barrier, inc=1, device_id={"dp": at_x(lax.rem(xc + t, NX))}, device_id_type=MESH
        )
        pl.semaphore_signal(
            barrier, inc=1, device_id={"dp": at_y(lax.rem(yc + t, NY))}, device_id_type=MESH
        )
    pl.semaphore_signal(barrier, inc=1, device_id={"dp": zmate}, device_id_type=MESH)

    @pl.when(xc != yc)
    def _():
        for z in range(NZ):
            pl.semaphore_signal(barrier, inc=1, device_id={"dp": turned(z)}, device_id_type=MESH)

    @pl.when(s > 0)
    def _():
        pl.semaphore_signal(barrier, inc=1, device_id={"section": s - 1}, device_id_type=MESH)

    @pl.when(s < last)
    def _():
        pl.semaphore_signal(barrier, inc=1, device_id={"section": s + 1}, device_id_type=MESH)

    def expand(exps, out):
        turn_v[...] = jnp.zeros_like(turn_v)
        for m in range(exps.shape[0]):
            for i in range(exps.shape[2]):
                own = exps[m, :, i, :]
                scale = jnp.left_shift(jnp.ones(own.shape, jnp.int32), own + 8).astype(F32) / 256.0
                at = (m * exps.shape[2] + i) * seq
                turn_v[: exps.shape[1], at : at + seq] = scale
        pad_v[...] = jnp.transpose(turn_v[...]).astype(BF16)

        def tile(k, carry):
            cols = pl.ds(pl.multiple_of(k * TW, TW), TW)
            block = lax.broadcasted_iota(jnp.int32, (pad_v.shape[1], TW), 0)
            lane = lax.broadcasted_iota(jnp.int32, (pad_v.shape[1], TW), 1)
            pick = (block == k * (TW // 128) + jnp.right_shift(lane, 7)).astype(F32).astype(BF16)
            out[:, cols] = dot_nn(pad_v[...], pick).astype(BF16)
            return carry

        lax.fori_loop(0, ntile, tile, 0)

    gg[...] = jnp.zeros_like(gg)
    acc_v[...] = jnp.zeros_like(acc_v)
    def transpose(source, out):
        def tile(k, carry):
            cols = pl.ds(pl.multiple_of(k * TW, TW), TW)
            out[:, cols] = jnp.transpose(source[cols, :])
            return carry

        lax.fori_loop(0, ntile, tile, 0)

    loads[0].wait()

    @pl.when(s < last)
    def _():
        expand(act_v, ascale)

    loads[2].wait()

    @pl.when(s < last)
    def _():
        transpose(up_v, up_t)

    loads[5].wait()

    @pl.when(s > 0)
    def _():
        expand(grad_v, gscale)

    loads[1].wait()
    loads[3].wait()

    @pl.when(s >= last - 1)
    def _():
        transpose(down_v, down_t)

    npeer = NX - 1 + NY - 1 + 1
    npeer = npeer + jnp.where(xc != yc, NZ, 0)
    pl.semaphore_wait(barrier, npeer + jnp.where(s > 0, 1, 0) + jnp.where(s < last, 1, 0))

    def send_x(c):
        return pltpu.make_async_remote_copy(
            src_ref=xout.at[rows_of(c)], dst_ref=x_st.at[rows_of(c)],
            send_sem=xs_sem.at[c], recv_sem=xin_sem.at[c],
            device_id={"section": s + 1}, device_id_type=MESH,
        )

    def send_dy(c):
        return pltpu.make_async_remote_copy(
            src_ref=dyout.at[rows_of(c)], dst_ref=dyb_st.at[rows_of(c)],
            send_sem=ds_sem.at[c], recv_sem=dy_sem.at[c],
            device_id={"section": s - 1}, device_id_type=MESH,
        )

    quarter = width // 4
    pair = nchunk // 4

    def quarters(kind, t, stash, out, rows, seg):
        other = lax.rem(mine[kind] + t, 4)
        cols = pl.ds(pl.multiple_of(other * quarter, 128), quarter)
        return pltpu.make_async_remote_copy(
            src_ref=stash.at[rows, cols], dst_ref=out.at[mine[kind], rows],
            send_sem=ex_send.at[kind, 0, t], recv_sem=ex_recv.at[kind, 0, seg, mine[kind]],
            device_id={"dp": ring_id(kind, other)}, device_id_type=MESH,
        )

    def units_of(kind, t, out, rows, seg):
        other = lax.rem(mine[kind] + t, 4)
        return pltpu.make_async_remote_copy(
            src_ref=out.at[mine[kind], rows], dst_ref=out.at[mine[kind], rows],
            send_sem=ex_send.at[kind, 1, t], recv_sem=ex_recv.at[kind, 1, seg, mine[kind]],
            device_id={"dp": ring_id(kind, other)}, device_id_type=MESH,
        )

    def own_quarter(kind, stash, out, rows, seg):
        cols = pl.ds(pl.multiple_of(mine[kind] * quarter, 128), quarter)
        return pltpu.make_async_copy(
            stash.at[rows, cols], out.at[mine[kind], rows], ex_recv.at[kind, 0, seg, mine[kind]]
        )

    def exchange(kind, stash, out, c):
        for t in (2, 1, 3):
            quarters(kind, t, stash, out, rows_of(c), lax.div(c, pair)).start()
        own_quarter(kind, stash, out, rows_of(c), lax.div(c, pair)).start()

    def exchange_units(kind, out, c):
        for t in (2, 1, 3):
            units_of(kind, t, out, rows_of(c), lax.div(c, pair)).start()

    def exchanged(kind, part, out, seg):
        rows = pl.ds(pl.multiple_of(seg * (pair * C), pair * C), pair * C)
        for t in range(1 if part else 0, 4):
            other = lax.rem(mine[kind] + t, 4)
            pltpu.make_async_copy(
                out.at[other, rows], out.at[other, rows], ex_recv.at[kind, part, seg, other]
            ).wait()

    def grads(kind, seg):
        data, units = ((xnq, dpq), (dybq, hq))[kind]
        exchanged(kind, 0, data, seg)
        exchanged(kind, 1, units, seg)
        rows = pl.ds(pl.multiple_of(seg * (pair * C), pair * C), pair * C)
        left = data[:, rows, :].reshape(4 * pair * C, quarter)
        right = units[:, rows, :].reshape(4 * pair * C, units.shape[2])
        acc_v[kind] += dot_tn(left, right)

    def cols_of(k):
        return pl.ds(pl.multiple_of(k * TW, TW), TW)

    def forward(c):
        rows = rows_of(c)
        pltpu.make_async_copy(x_st.at[rows], x_st.at[rows], xin_sem.at[c]).wait()

        def project(k, carry):
            squares, total = carry
            cols = cols_of(k)
            x = x_st[rows, cols].astype(F32)
            xg = (x * gain_v[:, cols]).astype(BF16)
            xn_st[rows, cols] = xg
            return squares + x * x, total + dot_nn(xg, down_v[cols, :])

        squares, total = lax.fori_loop(
            0, ntile, project,
            (jnp.zeros((C, TW), F32), jnp.zeros((C, down_v.shape[1]), F32)), unroll=True,
        )
        recip = lax.rsqrt(jnp.sum(squares, axis=1, keepdims=True) / width + EPS)
        r_st[rows, :] = jnp.broadcast_to(recip, (C, 128))
        pre = total * recip
        hidden = (pre * jax.nn.sigmoid(pre)).astype(BF16)
        p_st[rows, :] = pre
        hq[mine[1], rows, :] = hidden

        @pl.when(c == 0)
        def _():
            loads[4].wait()

        @pl.when(s < last)
        def _():
            slot = lax.div(c, per)
            pos = pl.ds(pl.multiple_of(lax.rem(c, per) * C, C), C)
            own = ids_ref[lax.div(slot, 2), lax.rem(slot, 2)] - dp * stored_v.shape[0]
            own = jnp.clip(own, 0, stored_v.shape[0] - 1)

            def code(k, carry):
                cols = cols_of(k)
                y = x_st[rows, cols].astype(F32) + dot_nn(hidden, up_t[:, cols])
                base = stored_v[own, pos, cols].astype(F32)
                scale = ascale[rows, cols].astype(F32)
                step = jnp.clip(y - base, -8.0 * scale, 7.0 * scale)
                xout[rows, cols] = (base + step).astype(BF16)
                return carry

            lax.fori_loop(0, ntile, code, 0, unroll=True)
            send_x(c).start()

        exchange(0, xn_st, xnq, c)
        exchange_units(1, hq, c)

    def backward(c):
        rows = rows_of(c)

        @pl.when(s < last)
        def _():
            pltpu.make_async_copy(dyb_st.at[rows], dyb_st.at[rows], dy_sem.at[c]).wait()

        @pl.when(s == 0)
        def _():
            exchange(1, dyb_st, dybq, c)

        dh = dot_nn(dyb_st[rows, :], up_v[...])
        pre = p_st[rows, :]
        sig = jax.nn.sigmoid(pre)
        dpre = (dh * sig * (1.0 + pre * (1.0 - sig))).astype(BF16)
        dpq[mine[0], rows, :] = (
            dpre.astype(F32) * jnp.concatenate([r_st[rows, :]] * (dpre.shape[1] // 128), axis=1)
        ).astype(BF16)
        exchange_units(0, dpq, c)
        wide = jnp.concatenate([r_st[rows, :]] * (TW // 128), axis=1)

        def first(k, acc):
            cols = cols_of(k)
            dxn = dot_nn(dpre, down_t[:, cols])
            ybuf[:, cols] = dxn
            prod = dxn * (x_st[rows, cols].astype(F32) * wide)
            gg[:, cols] += jnp.sum(prod.reshape(C // 8, 8, TW), axis=0)
            return acc + prod * gain_v[:, cols]

        acc = lax.fori_loop(0, ntile, first, jnp.zeros((C, TW), F32), unroll=True)

        @pl.when(s > 0)
        def _():
            mean = jnp.broadcast_to(jnp.sum(acc, axis=1, keepdims=True) / width, (C, TW)) * wide

            def second(k, carry):
                cols = cols_of(k)
                dz = ybuf[:, cols] * gain_v[:, cols]
                grad = wide * (dz - x_st[rows, cols].astype(F32) * mean) + dyb_st[rows, cols].astype(F32)
                scale = gscale[rows, cols].astype(F32)
                dyout[rows, cols] = jnp.clip(grad, -128.0 * scale, 127.0 * scale).astype(BF16)
                return carry

            lax.fori_loop(0, ntile, second, 0, unroll=True)
            send_dy(c).start()

            @pl.when(s < last)
            def _():
                exchange(1, dyb_st, dybq, c)

    @pl.when(s == last)
    def _():
        def early(c, carry):
            rows = rows_of(c)
            pltpu.make_async_copy(dyb_st.at[rows], dyb_st.at[rows], dy_sem.at[c]).wait()
            exchange(1, dyb_st, dybq, c)
            return carry

        lax.fori_loop(0, nchunk, early, 0)

    lag = jnp.where(s == last, 0, jnp.where(s == last - 1, 2, nchunk))

    def step(t, carry):
        @pl.when(t < nchunk)
        def _():
            forward(t)

        @pl.when((t == lag) & (s < last - 1))
        def _():
            transpose(down_v, down_t)

        done = t - lag

        early = (s < last - 1) & (done > pair) & (done < nchunk)

        @pl.when(early & (lax.rem(done, pair) == pair - 1))
        def _():
            for kind in (0, 1):
                grads(kind, lax.div(done, pair) - 1)

        @pl.when((t >= lag) & (t < lag + nchunk))
        def _():
            backward(t - lag)

        return carry

    lax.fori_loop(0, 2 * nchunk, step, 0)

    def gain_send(phase, t):
        coord, at = ((xc, at_x), (yc, at_y))[phase]
        return pltpu.make_async_remote_copy(
            src_ref=gx.at[phase, coord], dst_ref=gx.at[phase, coord],
            send_sem=gs_send.at[phase, t], recv_sem=gs_recv.at[phase, coord],
            device_id={"dp": at(lax.rem(coord + t, 4))}, device_id_type=MESH,
        )

    def gain_wait(phase):
        coord = (xc, yc)[phase]
        for t in range(1, 4):
            other = lax.rem(coord + t, 4)
            pltpu.make_async_copy(
                gx.at[phase, other], gx.at[phase, other], gs_recv.at[phase, other]
            ).wait()

    def gain_sum(phase):
        return (gx[phase, 0] + gx[phase, 1]) + (gx[phase, 2] + gx[phase, 3])

    def settle(kind, out):
        for a in range(2):
            value = acc_v[kind, :, a * 128 : (a + 1) * 128].astype(BF16)
            out[a] = value.reshape(NZ, NY, BR, 128)

    def ring_sends(kind, chunk, rel, frl):
        coord = cross[kind]
        right, left, opp = lax.rem(coord + 1, 4), lax.rem(coord + 3, 4), lax.rem(coord + 2, 4)

        def copy(i, src, dst, to):
            return pltpu.make_async_remote_copy(
                src_ref=src, dst_ref=dst,
                send_sem=rs_send.at[kind, i], recv_sem=rs_recv.at[kind, i],
                device_id={"dp": cross_id(kind, to)}, device_id_type=MESH,
            )

        return [
            copy(0, chunk(0, opp), rel.at[0], right),
            copy(1, chunk(1, opp), rel.at[1], left),
            copy(2, chunk(1, right), frl.at[0, 1], right),
            copy(3, chunk(0, left), frl.at[1, 0], left),
            copy(4, chunk(0, right), frl.at[0, 0], right),
            copy(5, chunk(1, left), frl.at[1, 1], left),
        ]

    sends = [
        ring_sends(0, lambda a, t: p1_0.at[a, :, t], rel2.at[0], frl2.at[0]),
        ring_sends(1, lambda a, t: p1_1.at[a, :, t], rel2.at[1], frl2.at[1]),
    ]

    def add(*refs):
        total = refs[0][...].astype(F32)
        for ref in refs[1:]:
            total = total + ref[...].astype(F32)
        return total

    def loop(n, body):
        def run(i, carry):
            body(i)
            return carry

        lax.fori_loop(0, n, run, 0)

    rings = ((p1_0, cross[0]), (p1_1, cross[1]))

    def begin(kind):
        grads(kind, 3)
        settle(kind, rings[kind][0])
        for i in range(4):
            sends[kind][i].start()

    def relay(kind):
        buf, coord = rings[kind]
        for a, to in ((0, lax.rem(coord + 1, 4)), (1, lax.rem(coord + 3, 4))):
            sends[kind][a].wait_recv()

            def body(v, a=a, to=to):
                buf[a, v, to] = add(buf.at[a, v, to], rel2.at[kind, a, v]).astype(BF16)

            loop(NZ, body)
            sends[kind][4 + a].start()

    def turn(kind, z):
        return pltpu.make_async_remote_copy(
            src_ref=q2.at[kind, z], dst_ref=qrecv.at[kind, zc],
            send_sem=q_send.at[kind, z], recv_sem=q_recv.at[kind, zc],
            device_id={"dp": owner(kind, z)}, device_id_type=MESH,
        )

    def finish(kind):
        buf, coord = rings[kind]
        for i in range(2, 6):
            sends[kind][i].wait_recv()
        for z in (1 - zc, zc):
            for a in range(2):
                q2[kind, z, a] = add(
                    buf.at[a, z, coord], frl2.at[kind, 0, a, z], frl2.at[kind, 1, a, z]
                ).astype(BF16)

            @pl.when(owner(kind, z) != dp)
            def _():
                turn(kind, z).start()

            @pl.when(owner(kind, z) == dp)
            def _():
                pltpu.make_async_copy(
                    q2.at[kind, z], qrecv.at[kind, zc], q_recv.at[kind, zc]
                ).start()

    @pl.when(s >= last - 1)
    def _():
        for kind in (0, 1):
            loop(3, functools.partial(grads, kind))

    begin(0)
    begin(1)

    nrow = width // 128
    for b in range(nrow):
        gx[0, xc, b : b + 1, :] = jnp.sum(gg[:, b * 128 : (b + 1) * 128], axis=0, keepdims=True)
    for t in range(1, 4):
        gain_send(0, t).start()
    relay(0)
    relay(1)
    gain_wait(0)
    gx[1, yc] = gain_sum(0)
    for t in range(1, 4):
        gain_send(1, t).start()
    finish(0)
    gain_wait(1)
    gx[2, zc] = gain_sum(1)
    zgain = pltpu.make_async_remote_copy(
        src_ref=gx.at[2, zc], dst_ref=gx.at[2, zc], send_sem=z_send.at[0], recv_sem=z_recv.at[0],
        device_id={"dp": zmate}, device_id_type=MESH,
    )
    zgain.start()
    finish(1)
    for kind, out in ((0, out_down), (1, out_up)):
        for z in range(NZ):
            pltpu.make_async_copy(
                qrecv.at[kind, z], qrecv.at[kind, z], q_recv.at[kind, z]
            ).wait()
        for a in range(2):
            out[:, a * 128 : (a + 1) * 128] = (
                add(qrecv.at[kind, 0, a], qrecv.at[kind, 1, a]) * factor
            )
    pltpu.make_async_copy(gx.at[2, 1 - zc], gx.at[2, 1 - zc], z_recv.at[0]).wait()
    out_gain[...] = (gx[2, 0] + gx[2, 1]) * factor

    zgain.wait_send()
    for kind in (0, 1):
        for z in range(NZ):

            @pl.when(owner(kind, z) != dp)
            def _():
                turn(kind, z).wait_send()

        for i in range(6):
            sends[kind][i].wait_send()
    every = pl.ds(0, tokens)
    for t in range(1, 4):
        quarters(0, t, xn_st, xnq, every, 0).wait_send()
        quarters(1, t, dyb_st, dybq, every, 0).wait_send()
        units_of(0, t, dpq, every, 0).wait_send()
        units_of(1, t, hq, every, 0).wait_send()
    for phase in (0, 1):
        for t in range(1, 4):
            gain_send(phase, t).wait_send()

    @pl.when(s < last)
    def _():
        loop(nchunk, lambda c: send_x(c).wait_send())

    @pl.when(s > 0)
    def _():
        loop(nchunk, lambda c: send_dy(c).wait_send())


def results(gain_ref, down_ref, up_ref, out_gain, out_down, out_up):
    for b in range(gain_ref.shape[0]):
        out_gain[:, b * 128 : (b + 1) * 128] = gain_ref[b : b + 1, :]
    out_down[0] = down_ref[...]
    out_up[0] = up_ref[...]


def local(inputs, cotangent, stored, sample_ids, act_exp, grad_exp, gain, down_weight, up_weight):
    micro, spm, seq, width = inputs.shape
    tokens = micro * spm * seq
    units = down_weight.shape[2]
    act_exp = jnp.transpose(act_exp, (0, 1, 4, 2, 3))
    grad_exp = jnp.transpose(grad_exp, (0, 1, 4, 2, 3))
    nchunk = tokens // C
    ndp = lax.axis_size("dp")
    factor = 1.0 / math.sqrt(tokens * ndp)
    hbm = pl.BlockSpec(memory_space=pl.ANY)
    vmem = pl.BlockSpec(memory_space=pltpu.VMEM)
    big = pltpu.VMEM((tokens, width), BF16)
    dma = pltpu.SemaphoreType.DMA
    scratch = [
        big, big, big, big, big,
        pltpu.VMEM((width, units), BF16), pltpu.VMEM((width, units), BF16),
        pltpu.VMEM(stored.shape[1:], BF16),
        big, big,
        pltpu.VMEM(act_exp.shape[1:], jnp.int32), pltpu.VMEM(grad_exp.shape[1:], jnp.int32),
        pltpu.VMEM((1, width), F32),
        pltpu.VMEM((128, tokens), F32),
        pltpu.VMEM((tokens, 128), BF16),
        pltpu.VMEM((tokens, 128), F32),
        pltpu.VMEM((tokens, units), F32),
        pltpu.VMEM((C, width), F32),
        pltpu.VMEM((8, width), F32),
        pltpu.VMEM((2, width // 4, units), F32),
        pltpu.VMEM((units, width), BF16), pltpu.VMEM((units, width), BF16),
        pltpu.VMEM((4, tokens, width // 4), BF16), pltpu.VMEM((4, tokens, width // 4), BF16),
        pltpu.VMEM((4, tokens, units), BF16), pltpu.VMEM((4, tokens, units), BF16),
        pltpu.VMEM((2, NZ, NY, BR, 128), BF16), pltpu.VMEM((2, NZ, NY, BR, 128), BF16),
        pltpu.VMEM((2, 2, NZ, BR, 128), BF16),
        pltpu.VMEM((2, 2, 2, NZ, BR, 128), BF16),
        pltpu.VMEM((2, 2, 2, BR, 128), BF16), pltpu.VMEM((2, 2, 2, BR, 128), BF16),
        pltpu.VMEM((3, 4, width // 128, 128), F32),
        dma((6,)), dma((nchunk,)), dma((nchunk,)), dma((nchunk,)), dma((nchunk,)),
        dma((2, 2, 4)), dma((2, 2, 4, 4)), dma((2, 6)), dma((2, 6)),
        dma((2, 4)), dma((2, 4)), dma((1,)), dma((1,)), dma((2, 2)), dma((2, 2)),
    ]
    outs = pl.pallas_call(
        functools.partial(kernel, factor),
        out_shape=(
            jax.ShapeDtypeStruct((width // 128, 128), F32),
            jax.ShapeDtypeStruct((BR, units), F32),
            jax.ShapeDtypeStruct((BR, units), F32),
        ),
        in_specs=[pl.BlockSpec(memory_space=pltpu.SMEM)] + [hbm] * 8,
        out_specs=(vmem, vmem, vmem),
        scratch_shapes=scratch,
        compiler_params=pltpu.CompilerParams(
            collective_id=0, has_side_effects=True, vmem_limit_bytes=60 * 1024 * 1024
        ),
    )(sample_ids, inputs, cotangent, stored, act_exp, grad_exp, gain, down_weight, up_weight)
    return pl.pallas_call(
        results,
        out_shape=(
            jax.ShapeDtypeStruct((1, width), F32),
            jax.ShapeDtypeStruct((1, BR, units), F32),
            jax.ShapeDtypeStruct((1, BR, units), F32),
        ),
        in_specs=[vmem] * 3,
        out_specs=(vmem, vmem, vmem),
    )(*outs)


def solution(mesh):
    placed = (
        P(None, "dp", None, None),
        P(None, "dp", None, None),
        P(None, "dp", None, None),
        P(None, "dp"),
        P(None, None, "dp", None, None),
        P(None, None, "dp", None, None),
        P("section", None),
        P("section", None, None),
        P("section", None, None),
    )
    return jax.shard_map(
        local,
        mesh=mesh,
        in_specs=placed,
        out_specs=(P("section", None), P("section", "dp", None), P("section", "dp", None)),
        check_vma=False,
    )
```

```python
import functools
import math

import jax
import jax.numpy as jnp
from jax import lax
from jax.experimental import pallas as pl
from jax.experimental.pallas import tpu as pltpu
from jax.sharding import PartitionSpec as P

EPS = 1e-05
MESH = pl.DeviceIdType.MESH
F32 = jnp.float32
BF16 = jnp.bfloat16
C = 32
TW = 512
NX, NZ, NY = 4, 2, 4
BR = 208


def dot_nn(a, b):
    return jnp.dot(a, b, preferred_element_type=F32)


def dot_tn(a, b):
    return lax.dot_general(a, b, (((0,), (0,)), ((), ())), preferred_element_type=F32)


def kernel(
    factor,
    ids_ref, inputs, cotangent, stored, act_exp, grad_exp, gain, down, up,
    out_gain, out_down, out_up,
    x_st, dyb_st, xn_st, xout, dyout, down_v, up_v, stored_v, ascale, gscale,
    act_v, grad_v, gain_v, turn_v, pad_v, r_st, p_st, ybuf, gg, acc_v, up_t, down_t,
    xnq, dybq, dpq, hq, p1_0, p1_1, rel2, frl2, q2, qrecv, gx,
    load_sem, xin_sem, xs_sem, dy_sem, ds_sem, ex_send, ex_recv, rs_send, rs_recv,
    gs_send, gs_recv, z_send, z_recv, q_send, q_recv,
):
    tokens, width = x_st.shape
    nchunk = tokens // C
    seq = inputs.shape[2]
    per = seq // C
    ntile = width // TW
    s = lax.axis_index("section")
    dp = lax.axis_index("dp")
    xc = lax.div(dp, NZ * NY)
    zc = lax.rem(lax.div(dp, NY), NZ)
    yc = lax.rem(dp, NY)
    last = lax.axis_size("section") - 1

    def at_x(t):
        return t * (NZ * NY) + zc * NY + yc

    def at_y(t):
        return xc * (NZ * NY) + zc * NY + t

    by_x = [s != last - 1, lax.rem(s, 2) == 0]
    mine = [jnp.where(by_x[kind], xc, yc) for kind in (0, 1)]
    cross = [jnp.where(by_x[kind], yc, xc) for kind in (0, 1)]

    def ring_id(kind, t):
        return jnp.where(by_x[kind], at_x(t), at_y(t))

    def cross_id(kind, t):
        return jnp.where(by_x[kind], at_y(t), at_x(t))

    def owner(kind, z):
        return mine[kind] * (NZ * NY) + z * NY + cross[kind]

    def turned(z):
        return yc * (NZ * NY) + z * NY + xc

    zmate = xc * (NZ * NY) + (1 - zc) * NY + yc

    loads = [
        pltpu.make_async_copy(act_exp.at[jnp.minimum(s, last - 1)], act_v, load_sem.at[0]),
        pltpu.make_async_copy(gain, gain_v, load_sem.at[1]),
        pltpu.make_async_copy(up.at[0], up_v, load_sem.at[2]),
        pltpu.make_async_copy(down.at[0], down_v, load_sem.at[3]),
        pltpu.make_async_copy(stored.at[jnp.minimum(s, last - 1)], stored_v, load_sem.at[4]),
        pltpu.make_async_copy(grad_exp.at[jnp.maximum(s - 1, 0)], grad_v, load_sem.at[5]),
    ]
    loads[0].start()
    loads[1].start()

    def rows_of(c):
        return pl.ds(pl.multiple_of(c * C, C), C)

    def own_rows(source, stash, sem, first, end):
        for c in range(first, end):
            slot = c // per
            pltpu.make_async_copy(
                source.at[slot // 2, slot % 2, pl.ds((c % per) * C, C)],
                stash.at[pl.ds(c * C, C)],
                sem.at[c],
            ).start()

    @pl.when(s == 0)
    def _():
        own_rows(inputs, x_st, xin_sem, 0, 1)

    for load in loads[2:]:
        load.start()

    @pl.when(s == 0)
    def _():
        own_rows(inputs, x_st, xin_sem, 1, nchunk)

    @pl.when(s == last)
    def _():
        own_rows(cotangent, dyb_st, dy_sem, 0, nchunk)

    barrier = pltpu.get_barrier_semaphore()
    for t in range(1, NX):
        pl.semaphore_signal(
            barrier, inc=1, device_id={"dp": at_x(lax.rem(xc + t, NX))}, device_id_type=MESH
        )
        pl.semaphore_signal(
            barrier, inc=1, device_id={"dp": at_y(lax.rem(yc + t, NY))}, device_id_type=MESH
        )
    pl.semaphore_signal(barrier, inc=1, device_id={"dp": zmate}, device_id_type=MESH)

    @pl.when(xc != yc)
    def _():
        for z in range(NZ):
            pl.semaphore_signal(barrier, inc=1, device_id={"dp": turned(z)}, device_id_type=MESH)

    @pl.when(s > 0)
    def _():
        pl.semaphore_signal(barrier, inc=1, device_id={"section": s - 1}, device_id_type=MESH)

    @pl.when(s < last)
    def _():
        pl.semaphore_signal(barrier, inc=1, device_id={"section": s + 1}, device_id_type=MESH)

    def expand(exps, out, first, count):
        turn_v[...] = jnp.zeros_like(turn_v)
        for m in range(exps.shape[0]):
            for i in range(exps.shape[2]):
                own = exps[m, :, i, :]
                scale = jnp.left_shift(jnp.ones(own.shape, jnp.int32), own + 8).astype(F32) / 256.0
                at = (m * exps.shape[2] + i) * seq
                turn_v[: exps.shape[1], at : at + seq] = scale
        pad_v[...] = jnp.transpose(turn_v[...]).astype(BF16)

        def tile(k, carry):
            cols = pl.ds(pl.multiple_of(k * TW, TW), TW)
            block = lax.broadcasted_iota(jnp.int32, (pad_v.shape[1], TW), 0)
            lane = lax.broadcasted_iota(jnp.int32, (pad_v.shape[1], TW), 1)
            pick = (block == k * (TW // 128) + jnp.right_shift(lane, 7)).astype(F32).astype(BF16)
            some = pl.ds(first, count)
            out[some, cols] = dot_nn(pad_v[some, :], pick).astype(BF16)
            return carry

        lax.fori_loop(0, ntile, tile, 0)

    gg[...] = jnp.zeros_like(gg)
    acc_v[...] = jnp.zeros_like(acc_v)
    def transpose(source, out):
        def tile(k, carry):
            cols = pl.ds(pl.multiple_of(k * TW, TW), TW)
            out[:, cols] = jnp.transpose(source[cols, :])
            return carry

        lax.fori_loop(0, ntile, tile, 0)

    loads[0].wait()

    @pl.when(s == 0)
    def _():
        expand(act_v, ascale, 0, 2 * C)

    @pl.when((s > 0) & (s < last))
    def _():
        expand(act_v, ascale, 0, tokens)

    loads[2].wait()

    @pl.when(s < last)
    def _():
        transpose(up_v, up_t)

    loads[5].wait()

    @pl.when(s > 0)
    def _():
        expand(grad_v, gscale, 0, tokens)

    loads[1].wait()
    loads[3].wait()

    @pl.when(s >= last - 1)
    def _():
        transpose(down_v, down_t)

    npeer = NX - 1 + NY - 1 + 1
    npeer = npeer + jnp.where(xc != yc, NZ, 0)
    pl.semaphore_wait(barrier, npeer + jnp.where(s > 0, 1, 0) + jnp.where(s < last, 1, 0))

    def send_x(c):
        return pltpu.make_async_remote_copy(
            src_ref=xout.at[rows_of(c)], dst_ref=x_st.at[rows_of(c)],
            send_sem=xs_sem.at[c], recv_sem=xin_sem.at[c],
            device_id={"section": s + 1}, device_id_type=MESH,
        )

    def send_dy(c):
        return pltpu.make_async_remote_copy(
            src_ref=dyout.at[rows_of(c)], dst_ref=dyb_st.at[rows_of(c)],
            send_sem=ds_sem.at[c], recv_sem=dy_sem.at[c],
            device_id={"section": s - 1}, device_id_type=MESH,
        )

    quarter = width // 4
    pair = nchunk // 4

    def quarters(kind, t, stash, out, rows, seg):
        other = lax.rem(mine[kind] + t, 4)
        cols = pl.ds(pl.multiple_of(other * quarter, 128), quarter)
        return pltpu.make_async_remote_copy(
            src_ref=stash.at[rows, cols], dst_ref=out.at[mine[kind], rows],
            send_sem=ex_send.at[kind, 0, t], recv_sem=ex_recv.at[kind, 0, seg, mine[kind]],
            device_id={"dp": ring_id(kind, other)}, device_id_type=MESH,
        )

    def units_of(kind, t, out, rows, seg):
        other = lax.rem(mine[kind] + t, 4)
        return pltpu.make_async_remote_copy(
            src_ref=out.at[mine[kind], rows], dst_ref=out.at[mine[kind], rows],
            send_sem=ex_send.at[kind, 1, t], recv_sem=ex_recv.at[kind, 1, seg, mine[kind]],
            device_id={"dp": ring_id(kind, other)}, device_id_type=MESH,
        )

    def own_quarter(kind, stash, out, rows, seg):
        cols = pl.ds(pl.multiple_of(mine[kind] * quarter, 128), quarter)
        return pltpu.make_async_copy(
            stash.at[rows, cols], out.at[mine[kind], rows], ex_recv.at[kind, 0, seg, mine[kind]]
        )

    def exchange(kind, stash, out, c):
        for t in (2, 1, 3):
            quarters(kind, t, stash, out, rows_of(c), lax.div(c, pair)).start()
        own_quarter(kind, stash, out, rows_of(c), lax.div(c, pair)).start()

    def exchange_units(kind, out, c):
        for t in (2, 1, 3):
            units_of(kind, t, out, rows_of(c), lax.div(c, pair)).start()

    def exchanged(kind, part, out, seg):
        rows = pl.ds(pl.multiple_of(seg * (pair * C), pair * C), pair * C)
        for t in range(1 if part else 0, 4):
            other = lax.rem(mine[kind] + t, 4)
            pltpu.make_async_copy(
                out.at[other, rows], out.at[other, rows], ex_recv.at[kind, part, seg, other]
            ).wait()

    def grads(kind, seg):
        data, units = ((xnq, dpq), (dybq, hq))[kind]
        exchanged(kind, 0, data, seg)
        exchanged(kind, 1, units, seg)
        rows = pl.ds(pl.multiple_of(seg * (pair * C), pair * C), pair * C)
        left = data[:, rows, :].reshape(4 * pair * C, quarter)
        right = units[:, rows, :].reshape(4 * pair * C, units.shape[2])
        acc_v[kind] += dot_tn(left, right)

    def cols_of(k):
        return pl.ds(pl.multiple_of(k * TW, TW), TW)

    def forward(c):
        rows = rows_of(c)
        pltpu.make_async_copy(x_st.at[rows], x_st.at[rows], xin_sem.at[c]).wait()

        def project(k, carry):
            squares, total = carry
            cols = cols_of(k)
            x = x_st[rows, cols].astype(F32)
            xg = (x * gain_v[:, cols]).astype(BF16)
            xn_st[rows, cols] = xg
            return squares + x * x, total + dot_nn(xg, down_v[cols, :])

        squares, total = lax.fori_loop(
            0, ntile, project,
            (jnp.zeros((C, TW), F32), jnp.zeros((C, down_v.shape[1]), F32)), unroll=True,
        )
        recip = lax.rsqrt(jnp.sum(squares, axis=1, keepdims=True) / width + EPS)
        r_st[rows, :] = jnp.broadcast_to(recip, (C, 128))
        pre = total * recip
        hidden = (pre * jax.nn.sigmoid(pre)).astype(BF16)
        p_st[rows, :] = pre
        hq[mine[1], rows, :] = hidden

        @pl.when(c == 0)
        def _():
            loads[4].wait()

        @pl.when(s < last)
        def _():
            slot = lax.div(c, per)
            pos = pl.ds(pl.multiple_of(lax.rem(c, per) * C, C), C)
            own = ids_ref[lax.div(slot, 2), lax.rem(slot, 2)] - dp * stored_v.shape[0]
            own = jnp.clip(own, 0, stored_v.shape[0] - 1)

            def code(k, carry):
                cols = cols_of(k)
                y = x_st[rows, cols].astype(F32) + dot_nn(hidden, up_t[:, cols])
                base = stored_v[own, pos, cols].astype(F32)
                scale = ascale[rows, cols].astype(F32)
                step = jnp.clip(y - base, -8.0 * scale, 7.0 * scale)
                xout[rows, cols] = (base + step).astype(BF16)
                return carry

            lax.fori_loop(0, ntile, code, 0, unroll=True)
            send_x(c).start()

        exchange(0, xn_st, xnq, c)
        exchange_units(1, hq, c)

    def backward(c):
        rows = rows_of(c)

        @pl.when(s < last)
        def _():
            pltpu.make_async_copy(dyb_st.at[rows], dyb_st.at[rows], dy_sem.at[c]).wait()

        @pl.when(s == 0)
        def _():
            exchange(1, dyb_st, dybq, c)

        dh = dot_nn(dyb_st[rows, :], up_v[...])
        pre = p_st[rows, :]
        sig = jax.nn.sigmoid(pre)
        dpre = (dh * sig * (1.0 + pre * (1.0 - sig))).astype(BF16)
        dpq[mine[0], rows, :] = (
            dpre.astype(F32) * jnp.concatenate([r_st[rows, :]] * (dpre.shape[1] // 128), axis=1)
        ).astype(BF16)
        exchange_units(0, dpq, c)
        wide = jnp.concatenate([r_st[rows, :]] * (TW // 128), axis=1)

        def first(k, acc):
            cols = cols_of(k)
            dxn = dot_nn(dpre, down_t[:, cols])
            ybuf[:, cols] = dxn
            prod = dxn * (x_st[rows, cols].astype(F32) * wide)
            gg[:, cols] += jnp.sum(prod.reshape(C // 8, 8, TW), axis=0)
            return acc + prod * gain_v[:, cols]

        acc = lax.fori_loop(0, ntile, first, jnp.zeros((C, TW), F32), unroll=True)

        @pl.when(s > 0)
        def _():
            mean = jnp.broadcast_to(jnp.sum(acc, axis=1, keepdims=True) / width, (C, TW)) * wide

            def second(k, carry):
                cols = cols_of(k)
                dz = ybuf[:, cols] * gain_v[:, cols]
                grad = wide * (dz - x_st[rows, cols].astype(F32) * mean) + dyb_st[rows, cols].astype(F32)
                scale = gscale[rows, cols].astype(F32)
                dyout[rows, cols] = jnp.clip(grad, -128.0 * scale, 127.0 * scale).astype(BF16)
                return carry

            lax.fori_loop(0, ntile, second, 0, unroll=True)
            send_dy(c).start()

            @pl.when(s < last)
            def _():
                exchange(1, dyb_st, dybq, c)

    @pl.when(s == last)
    def _():
        def early(c, carry):
            rows = rows_of(c)
            pltpu.make_async_copy(dyb_st.at[rows], dyb_st.at[rows], dy_sem.at[c]).wait()
            exchange(1, dyb_st, dybq, c)
            return carry

        lax.fori_loop(0, nchunk, early, 0)

    lag = jnp.where(s == last, 0, jnp.where(s == last - 1, 2, nchunk))

    def step(t, carry):
        @pl.when((t == 1) & (s == 0))
        def _():
            expand(act_v, ascale, 2 * C, tokens - 2 * C)

        @pl.when(t < nchunk)
        def _():
            forward(t)

        @pl.when((t == lag) & (s < last - 1))
        def _():
            transpose(down_v, down_t)

        done = t - lag

        early = (s < last - 1) & (done > pair) & (done < nchunk)

        @pl.when(early & (lax.rem(done, pair) == pair - 1))
        def _():
            for kind in (0, 1):
                grads(kind, lax.div(done, pair) - 1)

        @pl.when((t >= lag) & (t < lag + nchunk))
        def _():
            backward(t - lag)

        return carry

    lax.fori_loop(0, 2 * nchunk, step, 0)

    def gain_send(phase, t):
        coord, at = ((xc, at_x), (yc, at_y))[phase]
        return pltpu.make_async_remote_copy(
            src_ref=gx.at[phase, coord], dst_ref=gx.at[phase, coord],
            send_sem=gs_send.at[phase, t], recv_sem=gs_recv.at[phase, coord],
            device_id={"dp": at(lax.rem(coord + t, 4))}, device_id_type=MESH,
        )

    def gain_wait(phase):
        coord = (xc, yc)[phase]
        for t in range(1, 4):
            other = lax.rem(coord + t, 4)
            pltpu.make_async_copy(
                gx.at[phase, other], gx.at[phase, other], gs_recv.at[phase, other]
            ).wait()

    def gain_sum(phase):
        return (gx[phase, 0] + gx[phase, 1]) + (gx[phase, 2] + gx[phase, 3])

    def settle(kind, out):
        for a in range(2):
            value = acc_v[kind, :, a * 128 : (a + 1) * 128].astype(BF16)
            out[a] = value.reshape(NZ, NY, BR, 128)

    def ring_sends(kind, chunk, rel, frl):
        coord = cross[kind]
        right, left, opp = lax.rem(coord + 1, 4), lax.rem(coord + 3, 4), lax.rem(coord + 2, 4)

        def copy(i, src, dst, to):
            return pltpu.make_async_remote_copy(
                src_ref=src, dst_ref=dst,
                send_sem=rs_send.at[kind, i], recv_sem=rs_recv.at[kind, i],
                device_id={"dp": cross_id(kind, to)}, device_id_type=MESH,
            )

        return [
            copy(0, chunk(0, opp), rel.at[0], right),
            copy(1, chunk(1, opp), rel.at[1], left),
            copy(2, chunk(1, right), frl.at[0, 1], right),
            copy(3, chunk(0, left), frl.at[1, 0], left),
            copy(4, chunk(0, right), frl.at[0, 0], right),
            copy(5, chunk(1, left), frl.at[1, 1], left),
        ]

    sends = [
        ring_sends(0, lambda a, t: p1_0.at[a, :, t], rel2.at[0], frl2.at[0]),
        ring_sends(1, lambda a, t: p1_1.at[a, :, t], rel2.at[1], frl2.at[1]),
    ]

    def add(*refs):
        total = refs[0][...].astype(F32)
        for ref in refs[1:]:
            total = total + ref[...].astype(F32)
        return total

    def loop(n, body):
        def run(i, carry):
            body(i)
            return carry

        lax.fori_loop(0, n, run, 0)

    rings = ((p1_0, cross[0]), (p1_1, cross[1]))

    def begin(kind):
        grads(kind, 3)
        settle(kind, rings[kind][0])
        for i in range(4):
            sends[kind][i].start()

    def relay(kind):
        buf, coord = rings[kind]
        for a, to in ((0, lax.rem(coord + 1, 4)), (1, lax.rem(coord + 3, 4))):
            sends[kind][a].wait_recv()

            def body(v, a=a, to=to):
                buf[a, v, to] = add(buf.at[a, v, to], rel2.at[kind, a, v]).astype(BF16)

            loop(NZ, body)
            sends[kind][4 + a].start()

    def turn(kind, z):
        return pltpu.make_async_remote_copy(
            src_ref=q2.at[kind, z], dst_ref=qrecv.at[kind, zc],
            send_sem=q_send.at[kind, z], recv_sem=q_recv.at[kind, zc],
            device_id={"dp": owner(kind, z)}, device_id_type=MESH,
        )

    def finish(kind):
        buf, coord = rings[kind]
        for i in range(2, 6):
            sends[kind][i].wait_recv()
        for z in (1 - zc, zc):
            for a in range(2):
                q2[kind, z, a] = add(
                    buf.at[a, z, coord], frl2.at[kind, 0, a, z], frl2.at[kind, 1, a, z]
                ).astype(BF16)

            @pl.when(owner(kind, z) != dp)
            def _():
                turn(kind, z).start()

            @pl.when(owner(kind, z) == dp)
            def _():
                pltpu.make_async_copy(
                    q2.at[kind, z], qrecv.at[kind, zc], q_recv.at[kind, zc]
                ).start()

    @pl.when(s >= last - 1)
    def _():
        for kind in (0, 1):
            loop(3, functools.partial(grads, kind))

    begin(0)
    begin(1)

    nrow = width // 128
    for b in range(nrow):
        gx[0, xc, b : b + 1, :] = jnp.sum(gg[:, b * 128 : (b + 1) * 128], axis=0, keepdims=True)
    for t in range(1, 4):
        gain_send(0, t).start()
    relay(0)
    relay(1)
    gain_wait(0)
    gx[1, yc] = gain_sum(0)
    for t in range(1, 4):
        gain_send(1, t).start()
    finish(0)
    gain_wait(1)
    gx[2, zc] = gain_sum(1)
    zgain = pltpu.make_async_remote_copy(
        src_ref=gx.at[2, zc], dst_ref=gx.at[2, zc], send_sem=z_send.at[0], recv_sem=z_recv.at[0],
        device_id={"dp": zmate}, device_id_type=MESH,
    )
    zgain.start()
    finish(1)
    for kind, out in ((0, out_down), (1, out_up)):
        for z in range(NZ):
            pltpu.make_async_copy(
                qrecv.at[kind, z], qrecv.at[kind, z], q_recv.at[kind, z]
            ).wait()
        for a in range(2):
            out[:, a * 128 : (a + 1) * 128] = (
                add(qrecv.at[kind, 0, a], qrecv.at[kind, 1, a]) * factor
            )
    pltpu.make_async_copy(gx.at[2, 1 - zc], gx.at[2, 1 - zc], z_recv.at[0]).wait()
    out_gain[...] = (gx[2, 0] + gx[2, 1]) * factor

    zgain.wait_send()
    for kind in (0, 1):
        for z in range(NZ):

            @pl.when(owner(kind, z) != dp)
            def _():
                turn(kind, z).wait_send()

        for i in range(6):
            sends[kind][i].wait_send()
    every = pl.ds(0, tokens)
    for t in range(1, 4):
        quarters(0, t, xn_st, xnq, every, 0).wait_send()
        quarters(1, t, dyb_st, dybq, every, 0).wait_send()
        units_of(0, t, dpq, every, 0).wait_send()
        units_of(1, t, hq, every, 0).wait_send()
    for phase in (0, 1):
        for t in range(1, 4):
            gain_send(phase, t).wait_send()

    @pl.when(s < last)
    def _():
        loop(nchunk, lambda c: send_x(c).wait_send())

    @pl.when(s > 0)
    def _():
        loop(nchunk, lambda c: send_dy(c).wait_send())


def results(gain_ref, down_ref, up_ref, out_gain, out_down, out_up):
    for b in range(gain_ref.shape[0]):
        out_gain[:, b * 128 : (b + 1) * 128] = gain_ref[b : b + 1, :]
    out_down[0] = down_ref[...]
    out_up[0] = up_ref[...]


def local(inputs, cotangent, stored, sample_ids, act_exp, grad_exp, gain, down_weight, up_weight):
    micro, spm, seq, width = inputs.shape
    tokens = micro * spm * seq
    units = down_weight.shape[2]
    act_exp = jnp.transpose(act_exp, (0, 1, 4, 2, 3))
    grad_exp = jnp.transpose(grad_exp, (0, 1, 4, 2, 3))
    nchunk = tokens // C
    ndp = lax.axis_size("dp")
    factor = 1.0 / math.sqrt(tokens * ndp)
    hbm = pl.BlockSpec(memory_space=pl.ANY)
    vmem = pl.BlockSpec(memory_space=pltpu.VMEM)
    big = pltpu.VMEM((tokens, width), BF16)
    dma = pltpu.SemaphoreType.DMA
    scratch = [
        big, big, big, big, big,
        pltpu.VMEM((width, units), BF16), pltpu.VMEM((width, units), BF16),
        pltpu.VMEM(stored.shape[1:], BF16),
        big, big,
        pltpu.VMEM(act_exp.shape[1:], jnp.int32), pltpu.VMEM(grad_exp.shape[1:], jnp.int32),
        pltpu.VMEM((1, width), F32),
        pltpu.VMEM((128, tokens), F32),
        pltpu.VMEM((tokens, 128), BF16),
        pltpu.VMEM((tokens, 128), F32),
        pltpu.VMEM((tokens, units), F32),
        pltpu.VMEM((C, width), F32),
        pltpu.VMEM((8, width), F32),
        pltpu.VMEM((2, width // 4, units), F32),
        pltpu.VMEM((units, width), BF16), pltpu.VMEM((units, width), BF16),
        pltpu.VMEM((4, tokens, width // 4), BF16), pltpu.VMEM((4, tokens, width // 4), BF16),
        pltpu.VMEM((4, tokens, units), BF16), pltpu.VMEM((4, tokens, units), BF16),
        pltpu.VMEM((2, NZ, NY, BR, 128), BF16), pltpu.VMEM((2, NZ, NY, BR, 128), BF16),
        pltpu.VMEM((2, 2, NZ, BR, 128), BF16),
        pltpu.VMEM((2, 2, 2, NZ, BR, 128), BF16),
        pltpu.VMEM((2, 2, 2, BR, 128), BF16), pltpu.VMEM((2, 2, 2, BR, 128), BF16),
        pltpu.VMEM((3, 4, width // 128, 128), F32),
        dma((6,)), dma((nchunk,)), dma((nchunk,)), dma((nchunk,)), dma((nchunk,)),
        dma((2, 2, 4)), dma((2, 2, 4, 4)), dma((2, 6)), dma((2, 6)),
        dma((2, 4)), dma((2, 4)), dma((1,)), dma((1,)), dma((2, 2)), dma((2, 2)),
    ]
    outs = pl.pallas_call(
        functools.partial(kernel, factor),
        out_shape=(
            jax.ShapeDtypeStruct((width // 128, 128), F32),
            jax.ShapeDtypeStruct((BR, units), F32),
            jax.ShapeDtypeStruct((BR, units), F32),
        ),
        in_specs=[pl.BlockSpec(memory_space=pltpu.SMEM)] + [hbm] * 8,
        out_specs=(vmem, vmem, vmem),
        scratch_shapes=scratch,
        compiler_params=pltpu.CompilerParams(
            collective_id=0, has_side_effects=True, vmem_limit_bytes=60 * 1024 * 1024
        ),
    )(sample_ids, inputs, cotangent, stored, act_exp, grad_exp, gain, down_weight, up_weight)
    return pl.pallas_call(
        results,
        out_shape=(
            jax.ShapeDtypeStruct((1, width), F32),
            jax.ShapeDtypeStruct((1, BR, units), F32),
            jax.ShapeDtypeStruct((1, BR, units), F32),
        ),
        in_specs=[vmem] * 3,
        out_specs=(vmem, vmem, vmem),
    )(*outs)


def solution(mesh):
    placed = (
        P(None, "dp", None, None),
        P(None, "dp", None, None),
        P(None, "dp", None, None),
        P(None, "dp"),
        P(None, None, "dp", None, None),
        P(None, None, "dp", None, None),
        P("section", None),
        P("section", None, None),
        P("section", None, None),
    )
    return jax.shard_map(
        local,
        mesh=mesh,
        in_specs=placed,
        out_specs=(P("section", None), P("section", "dp", None), P("section", "dp", None)),
        check_vma=False,
    )
```

```python
import functools
import math

import jax
import jax.numpy as jnp
from jax import lax
from jax.experimental import pallas as pl
from jax.experimental.pallas import tpu as pltpu
from jax.sharding import PartitionSpec as P

EPS = 1e-05
MESH = pl.DeviceIdType.MESH
F32 = jnp.float32
BF16 = jnp.bfloat16
C = 32
TW = 512
NX, NZ, NY = 4, 2, 4
BR = 208


def dot_nn(a, b):
    return jnp.dot(a, b, preferred_element_type=F32)


def dot_tn(a, b):
    return lax.dot_general(a, b, (((0,), (0,)), ((), ())), preferred_element_type=F32)


def kernel(
    factor,
    ids_ref, inputs, cotangent, stored, act_exp, grad_exp, gain, down, up,
    out_gain, out_down, out_up,
    x_st, dyb_st, xn_st, xout, dyout, down_v, up_v, stored_v, ascale, gscale,
    act_v, grad_v, gain_v, turn_v, pad_v, r_st, p_st, ybuf, gg, acc_v, up_t, down_t,
    xnq, dybq, dpq, hq, p1_0, p1_1, rel2, frl2, q2, qrecv, gx,
    load_sem, xin_sem, xs_sem, dy_sem, ds_sem, ex_send, ex_recv, rs_send, rs_recv,
    gs_send, gs_recv, z_send, z_recv, q_send, q_recv,
):
    tokens, width = x_st.shape
    nchunk = tokens // C
    seq = inputs.shape[2]
    per = seq // C
    ntile = width // TW
    s = lax.axis_index("section")
    dp = lax.axis_index("dp")
    xc = lax.div(dp, NZ * NY)
    zc = lax.rem(lax.div(dp, NY), NZ)
    yc = lax.rem(dp, NY)
    last = lax.axis_size("section") - 1

    def at_x(t):
        return t * (NZ * NY) + zc * NY + yc

    def at_y(t):
        return xc * (NZ * NY) + zc * NY + t

    by_x = [s != last - 1, lax.rem(s, 2) == 0]
    mine = [jnp.where(by_x[kind], xc, yc) for kind in (0, 1)]
    cross = [jnp.where(by_x[kind], yc, xc) for kind in (0, 1)]

    def ring_id(kind, t):
        return jnp.where(by_x[kind], at_x(t), at_y(t))

    def cross_id(kind, t):
        return jnp.where(by_x[kind], at_y(t), at_x(t))

    def owner(kind, z):
        return mine[kind] * (NZ * NY) + z * NY + cross[kind]

    def turned(z):
        return yc * (NZ * NY) + z * NY + xc

    zmate = xc * (NZ * NY) + (1 - zc) * NY + yc

    loads = [
        pltpu.make_async_copy(act_exp.at[jnp.minimum(s, last - 1)], act_v, load_sem.at[0]),
        pltpu.make_async_copy(gain, gain_v, load_sem.at[1]),
        pltpu.make_async_copy(up.at[0], up_v, load_sem.at[2]),
        pltpu.make_async_copy(down.at[0], down_v, load_sem.at[3]),
        pltpu.make_async_copy(stored.at[jnp.minimum(s, last - 1)], stored_v, load_sem.at[4]),
        pltpu.make_async_copy(grad_exp.at[jnp.maximum(s - 1, 0)], grad_v, load_sem.at[5]),
    ]
    loads[0].start()
    loads[1].start()

    def rows_of(c):
        return pl.ds(pl.multiple_of(c * C, C), C)

    def own_rows(source, stash, sem, first, end):
        for c in range(first, end):
            slot = c // per
            pltpu.make_async_copy(
                source.at[slot // 2, slot % 2, pl.ds((c % per) * C, C)],
                stash.at[pl.ds(c * C, C)],
                sem.at[c],
            ).start()

    @pl.when(s == 0)
    def _():
        own_rows(inputs, x_st, xin_sem, 0, 1)

    for load in loads[2:]:
        load.start()

    @pl.when(s == 0)
    def _():
        own_rows(inputs, x_st, xin_sem, 1, nchunk)

    @pl.when(s == last)
    def _():
        own_rows(cotangent, dyb_st, dy_sem, 0, nchunk)

    barrier = pltpu.get_barrier_semaphore()
    for t in range(1, NX):
        pl.semaphore_signal(
            barrier, inc=1, device_id={"dp": at_x(lax.rem(xc + t, NX))}, device_id_type=MESH
        )
        pl.semaphore_signal(
            barrier, inc=1, device_id={"dp": at_y(lax.rem(yc + t, NY))}, device_id_type=MESH
        )
    pl.semaphore_signal(barrier, inc=1, device_id={"dp": zmate}, device_id_type=MESH)

    @pl.when(xc != yc)
    def _():
        for z in range(NZ):
            pl.semaphore_signal(barrier, inc=1, device_id={"dp": turned(z)}, device_id_type=MESH)

    @pl.when(s > 0)
    def _():
        pl.semaphore_signal(barrier, inc=1, device_id={"section": s - 1}, device_id_type=MESH)

    @pl.when(s < last)
    def _():
        pl.semaphore_signal(barrier, inc=1, device_id={"section": s + 1}, device_id_type=MESH)

    def expand(exps, out, first, count):
        turn_v[...] = jnp.zeros_like(turn_v)
        for m in range(exps.shape[0]):
            for i in range(exps.shape[2]):
                own = exps[m, :, i, :]
                scale = jnp.left_shift(jnp.ones(own.shape, jnp.int32), own + 8).astype(F32) / 256.0
                at = (m * exps.shape[2] + i) * seq
                turn_v[: exps.shape[1], at : at + seq] = scale
        pad_v[...] = jnp.transpose(turn_v[...]).astype(BF16)

        def tile(k, carry):
            cols = pl.ds(pl.multiple_of(k * TW, TW), TW)
            block = lax.broadcasted_iota(jnp.int32, (pad_v.shape[1], TW), 0)
            lane = lax.broadcasted_iota(jnp.int32, (pad_v.shape[1], TW), 1)
            pick = (block == k * (TW // 128) + jnp.right_shift(lane, 7)).astype(F32).astype(BF16)
            some = pl.ds(first, count)
            out[some, cols] = dot_nn(pad_v[some, :], pick).astype(BF16)
            return carry

        lax.fori_loop(0, ntile, tile, 0)

    gg[...] = jnp.zeros_like(gg)
    acc_v[...] = jnp.zeros_like(acc_v)
    def transpose(source, out):
        def tile(k, carry):
            cols = pl.ds(pl.multiple_of(k * TW, TW), TW)
            out[:, cols] = jnp.transpose(source[cols, :])
            return carry

        lax.fori_loop(0, ntile, tile, 0)

    loads[0].wait()

    @pl.when(s == 0)
    def _():
        expand(act_v, ascale, 0, 2 * C)

    @pl.when((s > 0) & (s < last))
    def _():
        expand(act_v, ascale, 0, tokens)

    loads[2].wait()

    @pl.when(s < last)
    def _():
        transpose(up_v, up_t)

    loads[5].wait()

    @pl.when(s > 0)
    def _():
        expand(grad_v, gscale, 0, tokens)

    loads[1].wait()
    loads[3].wait()

    @pl.when(s >= last - 1)
    def _():
        transpose(down_v, down_t)

    npeer = NX - 1 + NY - 1 + 1
    npeer = npeer + jnp.where(xc != yc, NZ, 0)
    pl.semaphore_wait(barrier, npeer + jnp.where(s > 0, 1, 0) + jnp.where(s < last, 1, 0))

    def send_x(c):
        return pltpu.make_async_remote_copy(
            src_ref=xout.at[rows_of(c)], dst_ref=x_st.at[rows_of(c)],
            send_sem=xs_sem.at[c], recv_sem=xin_sem.at[c],
            device_id={"section": s + 1}, device_id_type=MESH,
        )

    def send_dy(c):
        return pltpu.make_async_remote_copy(
            src_ref=dyout.at[rows_of(c)], dst_ref=dyb_st.at[rows_of(c)],
            send_sem=ds_sem.at[c], recv_sem=dy_sem.at[c],
            device_id={"section": s - 1}, device_id_type=MESH,
        )

    quarter = width // 4
    pair = nchunk // 4

    def quarters(kind, t, stash, out, rows, seg):
        other = lax.rem(mine[kind] + t, 4)
        cols = pl.ds(pl.multiple_of(other * quarter, 128), quarter)
        return pltpu.make_async_remote_copy(
            src_ref=stash.at[rows, cols], dst_ref=out.at[mine[kind], rows],
            send_sem=ex_send.at[kind, 0, t], recv_sem=ex_recv.at[kind, 0, seg, mine[kind]],
            device_id={"dp": ring_id(kind, other)}, device_id_type=MESH,
        )

    def units_of(kind, t, out, rows, seg):
        other = lax.rem(mine[kind] + t, 4)
        return pltpu.make_async_remote_copy(
            src_ref=out.at[mine[kind], rows], dst_ref=out.at[mine[kind], rows],
            send_sem=ex_send.at[kind, 1, t], recv_sem=ex_recv.at[kind, 1, seg, mine[kind]],
            device_id={"dp": ring_id(kind, other)}, device_id_type=MESH,
        )

    def own_quarter(kind, stash, out, rows, seg):
        cols = pl.ds(pl.multiple_of(mine[kind] * quarter, 128), quarter)
        return pltpu.make_async_copy(
            stash.at[rows, cols], out.at[mine[kind], rows], ex_recv.at[kind, 0, seg, mine[kind]]
        )

    def exchange(kind, stash, out, c):
        for t in (2, 1, 3):
            quarters(kind, t, stash, out, rows_of(c), lax.div(c, pair)).start()
        own_quarter(kind, stash, out, rows_of(c), lax.div(c, pair)).start()

    def exchange_units(kind, out, c):
        for t in (2, 1, 3):
            units_of(kind, t, out, rows_of(c), lax.div(c, pair)).start()

    def exchanged(kind, part, out, seg):
        rows = pl.ds(pl.multiple_of(seg * (pair * C), pair * C), pair * C)
        for t in range(1 if part else 0, 4):
            other = lax.rem(mine[kind] + t, 4)
            pltpu.make_async_copy(
                out.at[other, rows], out.at[other, rows], ex_recv.at[kind, part, seg, other]
            ).wait()

    def grads(kind, seg):
        data, units = ((xnq, dpq), (dybq, hq))[kind]
        exchanged(kind, 0, data, seg)
        exchanged(kind, 1, units, seg)
        rows = pl.ds(pl.multiple_of(seg * (pair * C), pair * C), pair * C)
        left = data[:, rows, :].reshape(4 * pair * C, quarter)
        right = units[:, rows, :].reshape(4 * pair * C, units.shape[2])
        acc_v[kind] += dot_tn(left, right)

    def cols_of(k):
        return pl.ds(pl.multiple_of(k * TW, TW), TW)

    def forward(c):
        rows = rows_of(c)
        pltpu.make_async_copy(x_st.at[rows], x_st.at[rows], xin_sem.at[c]).wait()

        def project(k, carry):
            squares, total = carry
            cols = cols_of(k)
            x = x_st[rows, cols].astype(F32)
            xg = (x * gain_v[:, cols]).astype(BF16)
            xn_st[rows, cols] = xg
            return squares + x * x, total + dot_nn(xg, down_v[cols, :])

        squares, total = lax.fori_loop(
            0, ntile, project,
            (jnp.zeros((C, TW), F32), jnp.zeros((C, down_v.shape[1]), F32)), unroll=True,
        )
        recip = lax.rsqrt(jnp.sum(squares, axis=1, keepdims=True) / width + EPS)
        r_st[rows, :] = jnp.broadcast_to(recip, (C, 128))
        pre = total * recip
        hidden = (pre * jax.nn.sigmoid(pre)).astype(BF16)
        p_st[rows, :] = pre
        hq[mine[1], rows, :] = hidden

        @pl.when(c == 0)
        def _():
            loads[4].wait()

        @pl.when(s < last)
        def _():
            slot = lax.div(c, per)
            pos = pl.ds(pl.multiple_of(lax.rem(c, per) * C, C), C)
            own = ids_ref[lax.div(slot, 2), lax.rem(slot, 2)] - dp * stored_v.shape[0]
            own = jnp.clip(own, 0, stored_v.shape[0] - 1)

            def code(k, carry):
                cols = cols_of(k)
                y = x_st[rows, cols].astype(F32) + dot_nn(hidden, up_t[:, cols])
                base = stored_v[own, pos, cols].astype(F32)
                scale = ascale[rows, cols].astype(F32)
                step = jnp.clip(y - base, -8.0 * scale, 7.0 * scale)
                xout[rows, cols] = (base + step).astype(BF16)
                return carry

            lax.fori_loop(0, ntile, code, 0, unroll=True)
            send_x(c).start()

        exchange(0, xn_st, xnq, c)
        exchange_units(1, hq, c)

    def backward(c):
        rows = rows_of(c)

        @pl.when(s < last)
        def _():
            pltpu.make_async_copy(dyb_st.at[rows], dyb_st.at[rows], dy_sem.at[c]).wait()

        @pl.when(s == 0)
        def _():
            exchange(1, dyb_st, dybq, c)

        dh = dot_nn(dyb_st[rows, :], up_v[...])
        pre = p_st[rows, :]
        sig = jax.nn.sigmoid(pre)
        dpre = (dh * sig * (1.0 + pre * (1.0 - sig))).astype(BF16)
        dpq[mine[0], rows, :] = (
            dpre.astype(F32) * jnp.concatenate([r_st[rows, :]] * (dpre.shape[1] // 128), axis=1)
        ).astype(BF16)
        exchange_units(0, dpq, c)
        wide = jnp.concatenate([r_st[rows, :]] * (TW // 128), axis=1)

        def first(k, acc):
            cols = cols_of(k)
            dxn = dot_nn(dpre, down_t[:, cols])
            ybuf[:, cols] = dxn
            prod = dxn * (x_st[rows, cols].astype(F32) * wide)
            gg[:, cols] += jnp.sum(prod.reshape(C // 8, 8, TW), axis=0)
            return acc + prod * gain_v[:, cols]

        acc = lax.fori_loop(0, ntile, first, jnp.zeros((C, TW), F32), unroll=True)

        @pl.when(s > 0)
        def _():
            mean = jnp.broadcast_to(jnp.sum(acc, axis=1, keepdims=True) / width, (C, TW)) * wide

            def second(k, carry):
                cols = cols_of(k)
                dz = ybuf[:, cols] * gain_v[:, cols]
                grad = wide * (dz - x_st[rows, cols].astype(F32) * mean) + dyb_st[rows, cols].astype(F32)
                scale = gscale[rows, cols].astype(F32)
                dyout[rows, cols] = jnp.clip(grad, -128.0 * scale, 127.0 * scale).astype(BF16)
                return carry

            lax.fori_loop(0, ntile, second, 0, unroll=True)
            send_dy(c).start()

            @pl.when(s < last)
            def _():
                exchange(1, dyb_st, dybq, c)

    @pl.when(s == last)
    def _():
        def early(c, carry):
            rows = rows_of(c)
            pltpu.make_async_copy(dyb_st.at[rows], dyb_st.at[rows], dy_sem.at[c]).wait()
            exchange(1, dyb_st, dybq, c)
            return carry

        lax.fori_loop(0, nchunk, early, 0)

    lag = jnp.where(s == last, 0, jnp.where(s == last - 1, 2, nchunk))

    def step(t, carry):
        @pl.when((t == 1) & (s == 0))
        def _():
            expand(act_v, ascale, 2 * C, tokens - 2 * C)

        @pl.when(t < nchunk)
        def _():
            forward(t)

        @pl.when((t == lag) & (s < last - 1))
        def _():
            transpose(down_v, down_t)

        done = t - lag

        early = (s < last - 1) & (done > pair) & (done < nchunk)

        @pl.when(early & (lax.rem(done, pair) == pair - 1))
        def _():
            for kind in (0, 1):
                grads(kind, lax.div(done, pair) - 1)

        @pl.when((t >= lag) & (t < lag + nchunk))
        def _():
            backward(t - lag)

        return carry

    lax.fori_loop(0, 2 * nchunk, step, 0)

    def gain_send(phase, t):
        coord, at = ((xc, at_x), (yc, at_y))[phase]
        return pltpu.make_async_remote_copy(
            src_ref=gx.at[phase, coord], dst_ref=gx.at[phase, coord],
            send_sem=gs_send.at[phase, t], recv_sem=gs_recv.at[phase, coord],
            device_id={"dp": at(lax.rem(coord + t, 4))}, device_id_type=MESH,
        )

    def gain_wait(phase):
        coord = (xc, yc)[phase]
        for t in range(1, 4):
            other = lax.rem(coord + t, 4)
            pltpu.make_async_copy(
                gx.at[phase, other], gx.at[phase, other], gs_recv.at[phase, other]
            ).wait()

    def gain_sum(phase):
        return (gx[phase, 0] + gx[phase, 1]) + (gx[phase, 2] + gx[phase, 3])

    def settle(kind, out):
        for a in range(2):
            value = acc_v[kind, :, a * 128 : (a + 1) * 128].astype(BF16)
            out[a] = value.reshape(NZ, NY, BR, 128)

    def ring_sends(kind, chunk, rel, frl):
        coord = cross[kind]
        right, left, opp = lax.rem(coord + 1, 4), lax.rem(coord + 3, 4), lax.rem(coord + 2, 4)

        def copy(i, src, dst, to):
            return pltpu.make_async_remote_copy(
                src_ref=src, dst_ref=dst,
                send_sem=rs_send.at[kind, i], recv_sem=rs_recv.at[kind, i],
                device_id={"dp": cross_id(kind, to)}, device_id_type=MESH,
            )

        return [
            copy(0, chunk(0, opp), rel.at[0], right),
            copy(1, chunk(1, opp), rel.at[1], left),
            copy(2, chunk(1, right), frl.at[0, 1], right),
            copy(3, chunk(0, left), frl.at[1, 0], left),
            copy(4, chunk(0, right), frl.at[0, 0], right),
            copy(5, chunk(1, left), frl.at[1, 1], left),
        ]

    sends = [
        ring_sends(0, lambda a, t: p1_0.at[a, :, t], rel2.at[0], frl2.at[0]),
        ring_sends(1, lambda a, t: p1_1.at[a, :, t], rel2.at[1], frl2.at[1]),
    ]

    def add(*refs):
        total = refs[0][...].astype(F32)
        for ref in refs[1:]:
            total = total + ref[...].astype(F32)
        return total

    def loop(n, body):
        def run(i, carry):
            body(i)
            return carry

        lax.fori_loop(0, n, run, 0)

    rings = ((p1_0, cross[0]), (p1_1, cross[1]))

    def begin(kind):
        grads(kind, 3)
        settle(kind, rings[kind][0])
        for i in range(4):
            sends[kind][i].start()

    def relay(kind):
        buf, coord = rings[kind]
        for a, to in ((0, lax.rem(coord + 1, 4)), (1, lax.rem(coord + 3, 4))):
            sends[kind][a].wait_recv()

            def body(v, a=a, to=to):
                buf[a, v, to] = add(buf.at[a, v, to], rel2.at[kind, a, v]).astype(BF16)

            loop(NZ, body)
            sends[kind][4 + a].start()

    def turn(kind, z):
        return pltpu.make_async_remote_copy(
            src_ref=q2.at[kind, z], dst_ref=qrecv.at[kind, zc],
            send_sem=q_send.at[kind, z], recv_sem=q_recv.at[kind, zc],
            device_id={"dp": owner(kind, z)}, device_id_type=MESH,
        )

    def finish(kind):
        buf, coord = rings[kind]
        for i in range(2, 6):
            sends[kind][i].wait_recv()
        for z in (1 - zc, zc):
            for a in range(2):
                q2[kind, z, a] = add(
                    buf.at[a, z, coord], frl2.at[kind, 0, a, z], frl2.at[kind, 1, a, z]
                ).astype(BF16)

            @pl.when(owner(kind, z) != dp)
            def _():
                turn(kind, z).start()

            @pl.when(owner(kind, z) == dp)
            def _():
                pltpu.make_async_copy(
                    q2.at[kind, z], qrecv.at[kind, zc], q_recv.at[kind, zc]
                ).start()

    @pl.when(s >= last - 1)
    def _():
        for kind in (0, 1):
            loop(3, functools.partial(grads, kind))

    nrow = width // 128
    for b in range(nrow):
        gx[0, xc, b : b + 1, :] = jnp.sum(gg[:, b * 128 : (b + 1) * 128], axis=0, keepdims=True)
    for t in range(1, 4):
        gain_send(0, t).start()
    begin(0)
    begin(1)
    gain_wait(0)
    gx[1, yc] = gain_sum(0)
    for t in range(1, 4):
        gain_send(1, t).start()

    relay(0)
    relay(1)
    gain_wait(1)
    gx[2, zc] = gain_sum(1)
    zgain = pltpu.make_async_remote_copy(
        src_ref=gx.at[2, zc], dst_ref=gx.at[2, zc], send_sem=z_send.at[0], recv_sem=z_recv.at[0],
        device_id={"dp": zmate}, device_id_type=MESH,
    )
    zgain.start()
    finish(0)
    finish(1)
    for kind, out in ((0, out_down), (1, out_up)):
        for z in range(NZ):
            pltpu.make_async_copy(
                qrecv.at[kind, z], qrecv.at[kind, z], q_recv.at[kind, z]
            ).wait()
        for a in range(2):
            out[:, a * 128 : (a + 1) * 128] = (
                add(qrecv.at[kind, 0, a], qrecv.at[kind, 1, a]) * factor
            )
    pltpu.make_async_copy(gx.at[2, 1 - zc], gx.at[2, 1 - zc], z_recv.at[0]).wait()
    out_gain[...] = (gx[2, 0] + gx[2, 1]) * factor

    zgain.wait_send()
    for kind in (0, 1):
        for z in range(NZ):

            @pl.when(owner(kind, z) != dp)
            def _():
                turn(kind, z).wait_send()

        for i in range(6):
            sends[kind][i].wait_send()
    every = pl.ds(0, tokens)
    for t in range(1, 4):
        quarters(0, t, xn_st, xnq, every, 0).wait_send()
        quarters(1, t, dyb_st, dybq, every, 0).wait_send()
        units_of(0, t, dpq, every, 0).wait_send()
        units_of(1, t, hq, every, 0).wait_send()
    for phase in (0, 1):
        for t in range(1, 4):
            gain_send(phase, t).wait_send()

    @pl.when(s < last)
    def _():
        loop(nchunk, lambda c: send_x(c).wait_send())

    @pl.when(s > 0)
    def _():
        loop(nchunk, lambda c: send_dy(c).wait_send())


def results(gain_ref, down_ref, up_ref, out_gain, out_down, out_up):
    for b in range(gain_ref.shape[0]):
        out_gain[:, b * 128 : (b + 1) * 128] = gain_ref[b : b + 1, :]
    out_down[0] = down_ref[...]
    out_up[0] = up_ref[...]


def local(inputs, cotangent, stored, sample_ids, act_exp, grad_exp, gain, down_weight, up_weight):
    micro, spm, seq, width = inputs.shape
    tokens = micro * spm * seq
    units = down_weight.shape[2]
    act_exp = jnp.transpose(act_exp, (0, 1, 4, 2, 3))
    grad_exp = jnp.transpose(grad_exp, (0, 1, 4, 2, 3))
    nchunk = tokens // C
    ndp = lax.axis_size("dp")
    factor = 1.0 / math.sqrt(tokens * ndp)
    hbm = pl.BlockSpec(memory_space=pl.ANY)
    vmem = pl.BlockSpec(memory_space=pltpu.VMEM)
    big = pltpu.VMEM((tokens, width), BF16)
    dma = pltpu.SemaphoreType.DMA
    scratch = [
        big, big, big, big, big,
        pltpu.VMEM((width, units), BF16), pltpu.VMEM((width, units), BF16),
        pltpu.VMEM(stored.shape[1:], BF16),
        big, big,
        pltpu.VMEM(act_exp.shape[1:], jnp.int32), pltpu.VMEM(grad_exp.shape[1:], jnp.int32),
        pltpu.VMEM((1, width), F32),
        pltpu.VMEM((128, tokens), F32),
        pltpu.VMEM((tokens, 128), BF16),
        pltpu.VMEM((tokens, 128), F32),
        pltpu.VMEM((tokens, units), F32),
        pltpu.VMEM((C, width), F32),
        pltpu.VMEM((8, width), F32),
        pltpu.VMEM((2, width // 4, units), F32),
        pltpu.VMEM((units, width), BF16), pltpu.VMEM((units, width), BF16),
        pltpu.VMEM((4, tokens, width // 4), BF16), pltpu.VMEM((4, tokens, width // 4), BF16),
        pltpu.VMEM((4, tokens, units), BF16), pltpu.VMEM((4, tokens, units), BF16),
        pltpu.VMEM((2, NZ, NY, BR, 128), BF16), pltpu.VMEM((2, NZ, NY, BR, 128), BF16),
        pltpu.VMEM((2, 2, NZ, BR, 128), BF16),
        pltpu.VMEM((2, 2, 2, NZ, BR, 128), BF16),
        pltpu.VMEM((2, 2, 2, BR, 128), BF16), pltpu.VMEM((2, 2, 2, BR, 128), BF16),
        pltpu.VMEM((3, 4, width // 128, 128), F32),
        dma((6,)), dma((nchunk,)), dma((nchunk,)), dma((nchunk,)), dma((nchunk,)),
        dma((2, 2, 4)), dma((2, 2, 4, 4)), dma((2, 6)), dma((2, 6)),
        dma((2, 4)), dma((2, 4)), dma((1,)), dma((1,)), dma((2, 2)), dma((2, 2)),
    ]
    outs = pl.pallas_call(
        functools.partial(kernel, factor),
        out_shape=(
            jax.ShapeDtypeStruct((width // 128, 128), F32),
            jax.ShapeDtypeStruct((BR, units), F32),
            jax.ShapeDtypeStruct((BR, units), F32),
        ),
        in_specs=[pl.BlockSpec(memory_space=pltpu.SMEM)] + [hbm] * 8,
        out_specs=(vmem, vmem, vmem),
        scratch_shapes=scratch,
        compiler_params=pltpu.CompilerParams(
            collective_id=0, has_side_effects=True, vmem_limit_bytes=60 * 1024 * 1024
        ),
    )(sample_ids, inputs, cotangent, stored, act_exp, grad_exp, gain, down_weight, up_weight)
    return pl.pallas_call(
        results,
        out_shape=(
            jax.ShapeDtypeStruct((1, width), F32),
            jax.ShapeDtypeStruct((1, BR, units), F32),
            jax.ShapeDtypeStruct((1, BR, units), F32),
        ),
        in_specs=[vmem] * 3,
        out_specs=(vmem, vmem, vmem),
    )(*outs)


def solution(mesh):
    placed = (
        P(None, "dp", None, None),
        P(None, "dp", None, None),
        P(None, "dp", None, None),
        P(None, "dp"),
        P(None, None, "dp", None, None),
        P(None, None, "dp", None, None),
        P("section", None),
        P("section", None, None),
        P("section", None, None),
    )
    return jax.shard_map(
        local,
        mesh=mesh,
        in_specs=placed,
        out_specs=(P("section", None), P("section", "dp", None), P("section", "dp", None)),
        check_vma=False,
    )
```

```python
import functools
import math

import jax
import jax.numpy as jnp
from jax import lax
from jax.experimental import pallas as pl
from jax.experimental.pallas import tpu as pltpu
from jax.sharding import PartitionSpec as P

EPS = 1e-05
MESH = pl.DeviceIdType.MESH
F32 = jnp.float32
BF16 = jnp.bfloat16
C = 32
TW = 512
NX, NZ, NY = 4, 2, 4
BR = 208


def dot_nn(a, b):
    return jnp.dot(a, b, preferred_element_type=F32)


def dot_tn(a, b):
    return lax.dot_general(a, b, (((0,), (0,)), ((), ())), preferred_element_type=F32)


def kernel(
    factor,
    ids_ref, inputs, cotangent, stored, act_exp, grad_exp, gain, down, up,
    out_gain, out_down, out_up,
    x_st, dyb_st, xn_st, xout, dyout, down_v, up_v, stored_v, ascale, gscale,
    act_v, grad_v, gain_v, turn_v, pad_v, r_st, p_st, ybuf, gg, acc_v, up_t, down_t,
    xnq, dybq, dpq, hq, p1_0, p1_1, rel2, frl2, q2, qrecv, gx,
    load_sem, xin_sem, xs_sem, dy_sem, ds_sem, ex_send, ex_recv, rs_send, rs_recv,
    gs_send, gs_recv, z_send, z_recv, q_send, q_recv,
):
    tokens, width = x_st.shape
    nchunk = tokens // C
    seq = inputs.shape[2]
    per = seq // C
    ntile = width // TW
    s = lax.axis_index("section")
    dp = lax.axis_index("dp")
    xc = lax.div(dp, NZ * NY)
    zc = lax.rem(lax.div(dp, NY), NZ)
    yc = lax.rem(dp, NY)
    last = lax.axis_size("section") - 1

    def at_x(t):
        return t * (NZ * NY) + zc * NY + yc

    def at_y(t):
        return xc * (NZ * NY) + zc * NY + t

    by_x = [s != last - 1, lax.rem(s, 2) == 0]
    mine = [jnp.where(by_x[kind], xc, yc) for kind in (0, 1)]
    cross = [jnp.where(by_x[kind], yc, xc) for kind in (0, 1)]

    def ring_id(kind, t):
        return jnp.where(by_x[kind], at_x(t), at_y(t))

    def cross_id(kind, t):
        return jnp.where(by_x[kind], at_y(t), at_x(t))

    def owner(kind, z):
        return mine[kind] * (NZ * NY) + z * NY + cross[kind]

    def turned(z):
        return yc * (NZ * NY) + z * NY + xc

    zmate = xc * (NZ * NY) + (1 - zc) * NY + yc

    loads = [
        pltpu.make_async_copy(act_exp.at[jnp.minimum(s, last - 1)], act_v, load_sem.at[0]),
        pltpu.make_async_copy(gain, gain_v, load_sem.at[1]),
        pltpu.make_async_copy(up.at[0], up_v, load_sem.at[2]),
        pltpu.make_async_copy(down.at[0], down_v, load_sem.at[3]),
        pltpu.make_async_copy(stored.at[jnp.minimum(s, last - 1)], stored_v, load_sem.at[4]),
        pltpu.make_async_copy(grad_exp.at[jnp.maximum(s - 1, 0)], grad_v, load_sem.at[5]),
    ]
    loads[0].start()
    loads[1].start()

    def rows_of(c):
        return pl.ds(pl.multiple_of(c * C, C), C)

    def own_rows(source, stash, sem, first, end):
        for c in range(first, end):
            slot = c // per
            pltpu.make_async_copy(
                source.at[slot // 2, slot % 2, pl.ds((c % per) * C, C)],
                stash.at[pl.ds(c * C, C)],
                sem.at[c],
            ).start()

    @pl.when(s == 0)
    def _():
        own_rows(inputs, x_st, xin_sem, 0, 1)

    for load in loads[2:]:
        load.start()

    @pl.when(s == 0)
    def _():
        own_rows(inputs, x_st, xin_sem, 1, nchunk)

    @pl.when(s == last)
    def _():
        own_rows(cotangent, dyb_st, dy_sem, 0, nchunk)

    barrier = pltpu.get_barrier_semaphore()
    for t in range(1, NX):
        pl.semaphore_signal(
            barrier, inc=1, device_id={"dp": at_x(lax.rem(xc + t, NX))}, device_id_type=MESH
        )
        pl.semaphore_signal(
            barrier, inc=1, device_id={"dp": at_y(lax.rem(yc + t, NY))}, device_id_type=MESH
        )
    pl.semaphore_signal(barrier, inc=1, device_id={"dp": zmate}, device_id_type=MESH)

    @pl.when(xc != yc)
    def _():
        for z in range(NZ):
            pl.semaphore_signal(barrier, inc=1, device_id={"dp": turned(z)}, device_id_type=MESH)

    @pl.when(s > 0)
    def _():
        pl.semaphore_signal(barrier, inc=1, device_id={"section": s - 1}, device_id_type=MESH)

    @pl.when(s < last)
    def _():
        pl.semaphore_signal(barrier, inc=1, device_id={"section": s + 1}, device_id_type=MESH)

    def expand(exps, out, first, count):
        turn_v[...] = jnp.zeros_like(turn_v)
        for m in range(exps.shape[0]):
            for i in range(exps.shape[2]):
                own = exps[m, :, i, :]
                scale = jnp.left_shift(jnp.ones(own.shape, jnp.int32), own + 8).astype(F32) / 256.0
                at = (m * exps.shape[2] + i) * seq
                turn_v[: exps.shape[1], at : at + seq] = scale
        pad_v[...] = jnp.transpose(turn_v[...]).astype(BF16)

        def tile(k, carry):
            cols = pl.ds(pl.multiple_of(k * TW, TW), TW)
            block = lax.broadcasted_iota(jnp.int32, (pad_v.shape[1], TW), 0)
            lane = lax.broadcasted_iota(jnp.int32, (pad_v.shape[1], TW), 1)
            pick = (block == k * (TW // 128) + jnp.right_shift(lane, 7)).astype(F32).astype(BF16)
            some = pl.ds(first, count)
            out[some, cols] = dot_nn(pad_v[some, :], pick).astype(BF16)
            return carry

        lax.fori_loop(0, ntile, tile, 0)

    gg[...] = jnp.zeros_like(gg)
    acc_v[...] = jnp.zeros_like(acc_v)
    def transpose(source, out):
        def tile(k, carry):
            cols = pl.ds(pl.multiple_of(k * TW, TW), TW)
            out[:, cols] = jnp.transpose(source[cols, :])
            return carry

        lax.fori_loop(0, ntile, tile, 0)

    loads[0].wait()

    @pl.when(s == 0)
    def _():
        expand(act_v, ascale, 0, 2 * C)

    @pl.when((s > 0) & (s < last))
    def _():
        expand(act_v, ascale, 0, tokens)

    loads[2].wait()

    @pl.when(s < last)
    def _():
        transpose(up_v, up_t)

    loads[5].wait()

    @pl.when(s > 0)
    def _():
        expand(grad_v, gscale, 0, tokens)

    loads[1].wait()
    loads[3].wait()

    @pl.when(s >= last - 1)
    def _():
        transpose(down_v, down_t)

    npeer = NX - 1 + NY - 1 + 1
    npeer = npeer + jnp.where(xc != yc, NZ, 0)
    pl.semaphore_wait(barrier, npeer + jnp.where(s > 0, 1, 0) + jnp.where(s < last, 1, 0))

    half = (ntile + 1) // 2
    whole = (0, ntile)
    parts = ((0, half), (half, ntile))

    def span(tiles):
        return pl.ds(tiles[0] * TW, (tiles[1] - tiles[0]) * TW)

    def send_x(c, tiles=whole):
        return pltpu.make_async_remote_copy(
            src_ref=xout.at[rows_of(c), span(tiles)], dst_ref=x_st.at[rows_of(c), span(tiles)],
            send_sem=xs_sem.at[c], recv_sem=xin_sem.at[c],
            device_id={"section": s + 1}, device_id_type=MESH,
        )

    def send_dy(c, tiles=whole):
        return pltpu.make_async_remote_copy(
            src_ref=dyout.at[rows_of(c), span(tiles)], dst_ref=dyb_st.at[rows_of(c), span(tiles)],
            send_sem=ds_sem.at[c], recv_sem=dy_sem.at[c],
            device_id={"section": s - 1}, device_id_type=MESH,
        )

    quarter = width // 4
    pair = nchunk // 4

    def quarters(kind, t, stash, out, rows, seg):
        other = lax.rem(mine[kind] + t, 4)
        cols = pl.ds(pl.multiple_of(other * quarter, 128), quarter)
        return pltpu.make_async_remote_copy(
            src_ref=stash.at[rows, cols], dst_ref=out.at[mine[kind], rows],
            send_sem=ex_send.at[kind, 0, t], recv_sem=ex_recv.at[kind, 0, seg, mine[kind]],
            device_id={"dp": ring_id(kind, other)}, device_id_type=MESH,
        )

    def units_of(kind, t, out, rows, seg):
        other = lax.rem(mine[kind] + t, 4)
        return pltpu.make_async_remote_copy(
            src_ref=out.at[mine[kind], rows], dst_ref=out.at[mine[kind], rows],
            send_sem=ex_send.at[kind, 1, t], recv_sem=ex_recv.at[kind, 1, seg, mine[kind]],
            device_id={"dp": ring_id(kind, other)}, device_id_type=MESH,
        )

    def own_quarter(kind, stash, out, rows, seg):
        cols = pl.ds(pl.multiple_of(mine[kind] * quarter, 128), quarter)
        return pltpu.make_async_copy(
            stash.at[rows, cols], out.at[mine[kind], rows], ex_recv.at[kind, 0, seg, mine[kind]]
        )

    def exchange(kind, stash, out, c):
        for t in (2, 1, 3):
            quarters(kind, t, stash, out, rows_of(c), lax.div(c, pair)).start()
        own_quarter(kind, stash, out, rows_of(c), lax.div(c, pair)).start()

    def exchange_units(kind, out, c):
        for t in (2, 1, 3):
            units_of(kind, t, out, rows_of(c), lax.div(c, pair)).start()

    def exchanged(kind, part, out, seg):
        rows = pl.ds(pl.multiple_of(seg * (pair * C), pair * C), pair * C)
        for t in range(1 if part else 0, 4):
            other = lax.rem(mine[kind] + t, 4)
            pltpu.make_async_copy(
                out.at[other, rows], out.at[other, rows], ex_recv.at[kind, part, seg, other]
            ).wait()

    def grads(kind, seg):
        data, units = ((xnq, dpq), (dybq, hq))[kind]
        exchanged(kind, 0, data, seg)
        exchanged(kind, 1, units, seg)
        rows = pl.ds(pl.multiple_of(seg * (pair * C), pair * C), pair * C)
        left = data[:, rows, :].reshape(4 * pair * C, quarter)
        right = units[:, rows, :].reshape(4 * pair * C, units.shape[2])
        acc_v[kind] += dot_tn(left, right)

    def cols_of(k):
        return pl.ds(pl.multiple_of(k * TW, TW), TW)

    def forward(c):
        rows = rows_of(c)
        pltpu.make_async_copy(x_st.at[rows], x_st.at[rows], xin_sem.at[c]).wait()

        def project(k, carry):
            squares, total = carry
            cols = cols_of(k)
            x = x_st[rows, cols].astype(F32)
            xg = (x * gain_v[:, cols]).astype(BF16)
            xn_st[rows, cols] = xg
            return squares + x * x, total + dot_nn(xg, down_v[cols, :])

        squares, total = lax.fori_loop(
            0, ntile, project,
            (jnp.zeros((C, TW), F32), jnp.zeros((C, down_v.shape[1]), F32)), unroll=True,
        )
        recip = lax.rsqrt(jnp.sum(squares, axis=1, keepdims=True) / width + EPS)
        r_st[rows, :] = jnp.broadcast_to(recip, (C, 128))
        pre = total * recip
        hidden = (pre * jax.nn.sigmoid(pre)).astype(BF16)
        p_st[rows, :] = pre
        hq[mine[1], rows, :] = hidden

        @pl.when(c == 0)
        def _():
            loads[4].wait()

        @pl.when(s < last)
        def _():
            slot = lax.div(c, per)
            pos = pl.ds(pl.multiple_of(lax.rem(c, per) * C, C), C)
            own = ids_ref[lax.div(slot, 2), lax.rem(slot, 2)] - dp * stored_v.shape[0]
            own = jnp.clip(own, 0, stored_v.shape[0] - 1)

            def code(k, carry):
                cols = cols_of(k)
                y = x_st[rows, cols].astype(F32) + dot_nn(hidden, up_t[:, cols])
                base = stored_v[own, pos, cols].astype(F32)
                scale = ascale[rows, cols].astype(F32)
                step = jnp.clip(y - base, -8.0 * scale, 7.0 * scale)
                xout[rows, cols] = (base + step).astype(BF16)
                return carry

            for tiles in parts:
                lax.fori_loop(*tiles, code, 0, unroll=True)
                send_x(c, tiles).start()

        exchange(0, xn_st, xnq, c)
        exchange_units(1, hq, c)

    def backward(c):
        rows = rows_of(c)

        @pl.when(s < last)
        def _():
            pltpu.make_async_copy(dyb_st.at[rows], dyb_st.at[rows], dy_sem.at[c]).wait()

        @pl.when(s == 0)
        def _():
            exchange(1, dyb_st, dybq, c)

        dh = dot_nn(dyb_st[rows, :], up_v[...])
        pre = p_st[rows, :]
        sig = jax.nn.sigmoid(pre)
        dpre = (dh * sig * (1.0 + pre * (1.0 - sig))).astype(BF16)
        dpq[mine[0], rows, :] = (
            dpre.astype(F32) * jnp.concatenate([r_st[rows, :]] * (dpre.shape[1] // 128), axis=1)
        ).astype(BF16)
        exchange_units(0, dpq, c)
        wide = jnp.concatenate([r_st[rows, :]] * (TW // 128), axis=1)

        def first(k, acc):
            cols = cols_of(k)
            dxn = dot_nn(dpre, down_t[:, cols])
            ybuf[:, cols] = dxn
            prod = dxn * (x_st[rows, cols].astype(F32) * wide)
            gg[:, cols] += jnp.sum(prod.reshape(C // 8, 8, TW), axis=0)
            return acc + prod * gain_v[:, cols]

        acc = lax.fori_loop(0, ntile, first, jnp.zeros((C, TW), F32), unroll=True)

        @pl.when(s > 0)
        def _():
            mean = jnp.broadcast_to(jnp.sum(acc, axis=1, keepdims=True) / width, (C, TW)) * wide

            def second(k, carry):
                cols = cols_of(k)
                dz = ybuf[:, cols] * gain_v[:, cols]
                grad = wide * (dz - x_st[rows, cols].astype(F32) * mean) + dyb_st[rows, cols].astype(F32)
                scale = gscale[rows, cols].astype(F32)
                dyout[rows, cols] = jnp.clip(grad, -128.0 * scale, 127.0 * scale).astype(BF16)
                return carry

            for tiles in parts:
                lax.fori_loop(*tiles, second, 0, unroll=True)
                send_dy(c, tiles).start()

            @pl.when(s < last)
            def _():
                exchange(1, dyb_st, dybq, c)

    @pl.when(s == last)
    def _():
        def early(c, carry):
            rows = rows_of(c)
            pltpu.make_async_copy(dyb_st.at[rows], dyb_st.at[rows], dy_sem.at[c]).wait()
            exchange(1, dyb_st, dybq, c)
            return carry

        lax.fori_loop(0, nchunk, early, 0)

    lag = jnp.where(s == last, 0, jnp.where(s == last - 1, 2, nchunk))

    def step(t, carry):
        @pl.when((t == 1) & (s == 0))
        def _():
            expand(act_v, ascale, 2 * C, tokens - 2 * C)

        @pl.when(t < nchunk)
        def _():
            forward(t)

        @pl.when((t == lag) & (s < last - 1))
        def _():
            transpose(down_v, down_t)

        done = t - lag

        early = (s < last - 1) & (done > pair) & (done < nchunk)

        @pl.when(early & (lax.rem(done, pair) == pair - 1))
        def _():
            for kind in (0, 1):
                grads(kind, lax.div(done, pair) - 1)

        @pl.when((t >= lag) & (t < lag + nchunk))
        def _():
            backward(t - lag)

        return carry

    lax.fori_loop(0, 2 * nchunk, step, 0)

    def gain_send(phase, t):
        coord, at = ((xc, at_x), (yc, at_y))[phase]
        return pltpu.make_async_remote_copy(
            src_ref=gx.at[phase, coord], dst_ref=gx.at[phase, coord],
            send_sem=gs_send.at[phase, t], recv_sem=gs_recv.at[phase, coord],
            device_id={"dp": at(lax.rem(coord + t, 4))}, device_id_type=MESH,
        )

    def gain_wait(phase):
        coord = (xc, yc)[phase]
        for t in range(1, 4):
            other = lax.rem(coord + t, 4)
            pltpu.make_async_copy(
                gx.at[phase, other], gx.at[phase, other], gs_recv.at[phase, other]
            ).wait()

    def gain_sum(phase):
        return (gx[phase, 0] + gx[phase, 1]) + (gx[phase, 2] + gx[phase, 3])

    def settle(kind, out):
        for a in range(2):
            value = acc_v[kind, :, a * 128 : (a + 1) * 128].astype(BF16)
            out[a] = value.reshape(NZ, NY, BR, 128)

    def ring_sends(kind, chunk, rel, frl):
        coord = cross[kind]
        right, left, opp = lax.rem(coord + 1, 4), lax.rem(coord + 3, 4), lax.rem(coord + 2, 4)

        def copy(i, src, dst, to):
            return pltpu.make_async_remote_copy(
                src_ref=src, dst_ref=dst,
                send_sem=rs_send.at[kind, i], recv_sem=rs_recv.at[kind, i],
                device_id={"dp": cross_id(kind, to)}, device_id_type=MESH,
            )

        return [
            copy(0, chunk(0, opp), rel.at[0], right),
            copy(1, chunk(1, opp), rel.at[1], left),
            copy(2, chunk(1, right), frl.at[0, 1], right),
            copy(3, chunk(0, left), frl.at[1, 0], left),
            copy(4, chunk(0, right), frl.at[0, 0], right),
            copy(5, chunk(1, left), frl.at[1, 1], left),
        ]

    sends = [
        ring_sends(0, lambda a, t: p1_0.at[a, :, t], rel2.at[0], frl2.at[0]),
        ring_sends(1, lambda a, t: p1_1.at[a, :, t], rel2.at[1], frl2.at[1]),
    ]

    def add(*refs):
        total = refs[0][...].astype(F32)
        for ref in refs[1:]:
            total = total + ref[...].astype(F32)
        return total

    def loop(n, body):
        def run(i, carry):
            body(i)
            return carry

        lax.fori_loop(0, n, run, 0)

    rings = ((p1_0, cross[0]), (p1_1, cross[1]))

    def begin(kind):
        grads(kind, 3)
        settle(kind, rings[kind][0])
        for i in range(4):
            sends[kind][i].start()

    def relay(kind):
        buf, coord = rings[kind]
        for a, to in ((0, lax.rem(coord + 1, 4)), (1, lax.rem(coord + 3, 4))):
            sends[kind][a].wait_recv()

            def body(v, a=a, to=to):
                buf[a, v, to] = add(buf.at[a, v, to], rel2.at[kind, a, v]).astype(BF16)

            loop(NZ, body)
            sends[kind][4 + a].start()

    def turn(kind, z):
        return pltpu.make_async_remote_copy(
            src_ref=q2.at[kind, z], dst_ref=qrecv.at[kind, zc],
            send_sem=q_send.at[kind, z], recv_sem=q_recv.at[kind, zc],
            device_id={"dp": owner(kind, z)}, device_id_type=MESH,
        )

    def finish(kind):
        buf, coord = rings[kind]
        for i in range(2, 6):
            sends[kind][i].wait_recv()
        for z in (1 - zc, zc):
            for a in range(2):
                q2[kind, z, a] = add(
                    buf.at[a, z, coord], frl2.at[kind, 0, a, z], frl2.at[kind, 1, a, z]
                ).astype(BF16)

            @pl.when(owner(kind, z) != dp)
            def _():
                turn(kind, z).start()

            @pl.when(owner(kind, z) == dp)
            def _():
                pltpu.make_async_copy(
                    q2.at[kind, z], qrecv.at[kind, zc], q_recv.at[kind, zc]
                ).start()

    @pl.when(s >= last - 1)
    def _():
        for kind in (0, 1):
            loop(3, functools.partial(grads, kind))

    nrow = width // 128
    for b in range(nrow):
        gx[0, xc, b : b + 1, :] = jnp.sum(gg[:, b * 128 : (b + 1) * 128], axis=0, keepdims=True)
    for t in range(1, 4):
        gain_send(0, t).start()
    begin(0)
    begin(1)
    gain_wait(0)
    gx[1, yc] = gain_sum(0)
    for t in range(1, 4):
        gain_send(1, t).start()

    relay(0)
    relay(1)
    gain_wait(1)
    gx[2, zc] = gain_sum(1)
    zgain = pltpu.make_async_remote_copy(
        src_ref=gx.at[2, zc], dst_ref=gx.at[2, zc], send_sem=z_send.at[0], recv_sem=z_recv.at[0],
        device_id={"dp": zmate}, device_id_type=MESH,
    )
    zgain.start()
    finish(0)
    finish(1)
    for kind, out in ((0, out_down), (1, out_up)):
        for z in range(NZ):
            pltpu.make_async_copy(
                qrecv.at[kind, z], qrecv.at[kind, z], q_recv.at[kind, z]
            ).wait()
        for a in range(2):
            out[:, a * 128 : (a + 1) * 128] = (
                add(qrecv.at[kind, 0, a], qrecv.at[kind, 1, a]) * factor
            )
    pltpu.make_async_copy(gx.at[2, 1 - zc], gx.at[2, 1 - zc], z_recv.at[0]).wait()
    out_gain[...] = (gx[2, 0] + gx[2, 1]) * factor

    zgain.wait_send()
    for kind in (0, 1):
        for z in range(NZ):

            @pl.when(owner(kind, z) != dp)
            def _():
                turn(kind, z).wait_send()

        for i in range(6):
            sends[kind][i].wait_send()
    every = pl.ds(0, tokens)
    for t in range(1, 4):
        quarters(0, t, xn_st, xnq, every, 0).wait_send()
        quarters(1, t, dyb_st, dybq, every, 0).wait_send()
        units_of(0, t, dpq, every, 0).wait_send()
        units_of(1, t, hq, every, 0).wait_send()
    for phase in (0, 1):
        for t in range(1, 4):
            gain_send(phase, t).wait_send()

    @pl.when(s < last)
    def _():
        loop(nchunk, lambda c: send_x(c).wait_send())

    @pl.when(s > 0)
    def _():
        loop(nchunk, lambda c: send_dy(c).wait_send())


def results(gain_ref, down_ref, up_ref, out_gain, out_down, out_up):
    for b in range(gain_ref.shape[0]):
        out_gain[:, b * 128 : (b + 1) * 128] = gain_ref[b : b + 1, :]
    out_down[0] = down_ref[...]
    out_up[0] = up_ref[...]


def local(inputs, cotangent, stored, sample_ids, act_exp, grad_exp, gain, down_weight, up_weight):
    micro, spm, seq, width = inputs.shape
    tokens = micro * spm * seq
    units = down_weight.shape[2]
    act_exp = jnp.transpose(act_exp, (0, 1, 4, 2, 3))
    grad_exp = jnp.transpose(grad_exp, (0, 1, 4, 2, 3))
    nchunk = tokens // C
    ndp = lax.axis_size("dp")
    factor = 1.0 / math.sqrt(tokens * ndp)
    hbm = pl.BlockSpec(memory_space=pl.ANY)
    vmem = pl.BlockSpec(memory_space=pltpu.VMEM)
    big = pltpu.VMEM((tokens, width), BF16)
    dma = pltpu.SemaphoreType.DMA
    scratch = [
        big, big, big, big, big,
        pltpu.VMEM((width, units), BF16), pltpu.VMEM((width, units), BF16),
        pltpu.VMEM(stored.shape[1:], BF16),
        big, big,
        pltpu.VMEM(act_exp.shape[1:], jnp.int32), pltpu.VMEM(grad_exp.shape[1:], jnp.int32),
        pltpu.VMEM((1, width), F32),
        pltpu.VMEM((128, tokens), F32),
        pltpu.VMEM((tokens, 128), BF16),
        pltpu.VMEM((tokens, 128), F32),
        pltpu.VMEM((tokens, units), F32),
        pltpu.VMEM((C, width), F32),
        pltpu.VMEM((8, width), F32),
        pltpu.VMEM((2, width // 4, units), F32),
        pltpu.VMEM((units, width), BF16), pltpu.VMEM((units, width), BF16),
        pltpu.VMEM((4, tokens, width // 4), BF16), pltpu.VMEM((4, tokens, width // 4), BF16),
        pltpu.VMEM((4, tokens, units), BF16), pltpu.VMEM((4, tokens, units), BF16),
        pltpu.VMEM((2, NZ, NY, BR, 128), BF16), pltpu.VMEM((2, NZ, NY, BR, 128), BF16),
        pltpu.VMEM((2, 2, NZ, BR, 128), BF16),
        pltpu.VMEM((2, 2, 2, NZ, BR, 128), BF16),
        pltpu.VMEM((2, 2, 2, BR, 128), BF16), pltpu.VMEM((2, 2, 2, BR, 128), BF16),
        pltpu.VMEM((3, 4, width // 128, 128), F32),
        dma((6,)), dma((nchunk,)), dma((nchunk,)), dma((nchunk,)), dma((nchunk,)),
        dma((2, 2, 4)), dma((2, 2, 4, 4)), dma((2, 6)), dma((2, 6)),
        dma((2, 4)), dma((2, 4)), dma((1,)), dma((1,)), dma((2, 2)), dma((2, 2)),
    ]
    outs = pl.pallas_call(
        functools.partial(kernel, factor),
        out_shape=(
            jax.ShapeDtypeStruct((width // 128, 128), F32),
            jax.ShapeDtypeStruct((BR, units), F32),
            jax.ShapeDtypeStruct((BR, units), F32),
        ),
        in_specs=[pl.BlockSpec(memory_space=pltpu.SMEM)] + [hbm] * 8,
        out_specs=(vmem, vmem, vmem),
        scratch_shapes=scratch,
        compiler_params=pltpu.CompilerParams(
            collective_id=0, has_side_effects=True, vmem_limit_bytes=60 * 1024 * 1024
        ),
    )(sample_ids, inputs, cotangent, stored, act_exp, grad_exp, gain, down_weight, up_weight)
    return pl.pallas_call(
        results,
        out_shape=(
            jax.ShapeDtypeStruct((1, width), F32),
            jax.ShapeDtypeStruct((1, BR, units), F32),
            jax.ShapeDtypeStruct((1, BR, units), F32),
        ),
        in_specs=[vmem] * 3,
        out_specs=(vmem, vmem, vmem),
    )(*outs)


def solution(mesh):
    placed = (
        P(None, "dp", None, None),
        P(None, "dp", None, None),
        P(None, "dp", None, None),
        P(None, "dp"),
        P(None, None, "dp", None, None),
        P(None, None, "dp", None, None),
        P("section", None),
        P("section", None, None),
        P("section", None, None),
    )
    return jax.shard_map(
        local,
        mesh=mesh,
        in_specs=placed,
        out_specs=(P("section", None), P("section", "dp", None), P("section", "dp", None)),
        check_vma=False,
    )
```
